256 devices in a mesh: space: 64 (over y, z, core), coil: 4 (over x).
Axes of the slice: x: 4, y: 4, z: 8, core: 2. Of those that a mesh axis runs over, the one named last changes fastest.
Arguments:
- k_space: bfloat16 [2, 16, 256, 64, 320], P(None, 'coil', 'space'), may hold values from -6 to 6
- cotangent: bfloat16 [2, 16, 256, 64, 320], P(None, 'coil', 'space'), may hold values from -6 to 6
- sens_maps: bfloat16 [2, 16, 256, 64, 320], P(None, 'coil', None, 'space'), may hold values from -0.75 to 0.75
- line_index: int32 [256, 40], replicated, may hold values from 0 to 319, all different within a row
- w_first: bfloat16 [18, 2, 3, 3], replicated, may hold values from -1.5 to 1.5
- b_first: float32 [18], replicated, may hold values from -3 to 3
- w_second: bfloat16 [2, 18, 3, 3], replicated, may hold values from -0.5 to 0.5
- b_second: float32 [2], replicated, may hold values from -3 to 3
Outputs:
- grad_sens: bfloat16 [2, 16, 256, 64, 320], P(None, 'coil', None, 'space')
- grad_w1: float32 [18, 2, 3, 3], replicated
- grad_b1: float32 [18], replicated
- grad_w2: float32 [2, 18, 3, 3], replicated
- grad_b2: float32 [2], replicated
The draws below stay inside these ranges and needn't reach their ends.
Inputs may be any that keep to these rules, and one draw needn't show every extreme that they name: Each row of line_index lists 40 different phase-encode indices.
All inputs are finite; a program needn't handle non-finite values.
Results may differ from the reference program's by a relative error of at most 0.04.
Values may be sent and summed in bfloat16 or wider, within the bound.
A program may use at most 320 MiB of HBM per device.

```python
import math
import jax
import jax.numpy as jnp
from jax import lax

C = 16
NY = 320
NZ = 256
CH = 18
NX = 64
LINES = 40


def shard_levels(stream_key, shape, split, smallest, top_value):
    gain = 1.0
    for axis_at, blocks in split:
        draws = jax.random.uniform(jax.random.fold_in(jax.random.fold_in(stream_key, 6), axis_at), (blocks,), jnp.float32, smallest / len(split), top_value / len(split))
        gain = gain * jnp.repeat(jnp.exp(draws), shape[axis_at] // blocks).reshape((-1,) + (1,) * (len(shape) - 1 - axis_at))
    return gain


def choose_distinct(own_key, rows, count, top, lift):
    ranking = jax.random.permutation(jax.random.fold_in(own_key, 1), count)
    boost = ranking
    for power in range(3):
        boost = boost * boost // count
    boost = boost * lift // count
    tickets = jax.random.randint(jax.random.fold_in(own_key, 2), (rows, count), 0, 4096) + boost
    holders = jax.random.permutation(jax.random.fold_in(own_key, 3), rows)[jnp.arange(count) % rows]
    tickets = jnp.where(jnp.arange(rows)[:, None] == holders[None, :], 1 << 14, tickets)
    merit = tickets * count + jnp.arange(count)
    return lax.top_k(merit.astype(jnp.int32), top)[1].astype(jnp.int32)


def normal_values(rng, dims, deviation, bound, cuts=(), kind=jnp.bfloat16):
    result = deviation * jax.random.normal(rng, dims, jnp.float32)
    if cuts:
        result = result * shard_levels(rng, dims, cuts, -0.22, 0.18)
    return jnp.clip(result, -bound, bound).astype(kind)


def setup_inputs(seed: int = 0) -> dict:
    keys = jax.random.split(jax.random.key(seed), 9)
    k_space = normal_values(keys[0], (2, C, NZ, NX, NY), 1.0, 6.0, ((1, 4), (2, 64)))
    cotangent = normal_values(keys[1], (2, C, NZ, NX, NY), 1.0, 6.0, ((1, 4), (2, 64)))
    sens_maps = normal_values(keys[2], (2, C, NZ, NX, NY), 0.125, 0.75, ((1, 4), (3, 64)))
    line_index = choose_distinct(keys[3], NZ, NY, LINES, 0)
    w_first = normal_values(keys[4], (CH, 2, 3, 3), 18 ** -0.5, 1.5)
    b_first = normal_values(keys[5], (CH,), 0.5, 3.0, (), jnp.float32)
    w_second = normal_values(keys[6], (2, CH, 3, 3), (CH * 9) ** -0.5, 0.5)
    b_second = normal_values(keys[7], (2,), 0.5, 3.0, (), jnp.float32)
    return dict(k_space=k_space, cotangent=cotangent, sens_maps=sens_maps, line_index=line_index, w_first=w_first, b_first=b_first, w_second=w_second, b_second=b_second)


def dft_table(length):
    position = jnp.arange(length, dtype=jnp.int32)
    product = position[:, None] * position[None, :] % length
    angles = 2.0 * math.pi / length * product.astype(jnp.float32)
    scaling = 1.0 / math.sqrt(length)
    cosine = jnp.cos(angles) * scaling
    sine_part = jnp.sin(angles) * scaling
    return jnp.stack([jnp.stack([cosine, sine_part]), jnp.stack([-sine_part, cosine])]).astype(jnp.bfloat16)

def plane_conv(padded, kernel):
    return lax.conv_general_dilated(padded, kernel, (1, 1), ((0, 0), (1, 1)), dimension_numbers=('CNHW', 'OIHW', 'CNHW'), preferred_element_type=jnp.float32)

def flip_kernel(kernel):
    return jnp.transpose(kernel[:, :, ::-1, ::-1], (1, 0, 2, 3))

def kernel_grad(cot_array, padded):
    widened = jnp.pad(padded, ((0, 0), (0, 0), (0, 0), (1, 1)))
    len_x = cot_array.shape[2]
    len_y = cot_array.shape[3]
    row_list = []
    for shift_x in range(3):
        for shift_y in range(3):
            window = widened[:, :, shift_x:shift_x + len_x, shift_y:shift_y + len_y]
            row_list.append(jnp.einsum('ozxy,izxy->oi', cot_array.astype(jnp.float32), window.astype(jnp.float32)))
    return jnp.stack(row_list, axis=2).reshape(cot_array.shape[0], padded.shape[0], 3, 3)

def regularize(combined, grad_reg, w_first, b_first, w_second, b_second, extend):
    comb_pad = extend(combined)
    hidden_pre = plane_conv(comb_pad, w_first) + b_first[:, None, None, None]
    activation = jax.nn.silu(hidden_pre).astype(jnp.bfloat16)
    act_pad = extend(activation)
    regularized = (plane_conv(act_pad, w_second) + b_second[:, None, None, None]).astype(jnp.bfloat16)
    grad_act = plane_conv(extend(grad_reg), flip_kernel(w_second))
    logistic = jax.nn.sigmoid(hidden_pre)
    grad_pre = (grad_act * logistic * (1.0 + hidden_pre * (1.0 - logistic))).astype(jnp.bfloat16)
    grad_comb = plane_conv(extend(grad_pre), flip_kernel(w_first)).astype(jnp.bfloat16)
    weight_grads = (kernel_grad(grad_pre, comb_pad), lax.optimization_barrier(jnp.sum(grad_pre.astype(jnp.float32), axis=(1, 2, 3))), kernel_grad(grad_reg, act_pad), lax.optimization_barrier(jnp.sum(grad_reg.astype(jnp.float32), axis=(1, 2, 3))))
    return (regularized, grad_comb, weight_grads)

def reference(k_space, cotangent, sens_maps, line_index, w_first, b_first, w_second, b_second):
    table_y = dft_table(NY)
    table_z = dft_table(NZ)
    sampled = jnp.any(line_index[:, :, None] == jnp.arange(NY, dtype=jnp.int32)[None, None, :], axis=1).astype(jnp.bfloat16)

    def inverse_volume(spectrum):
        half_image = jnp.einsum('pzxk,pqky->qzxy', spectrum.astype(jnp.float32), table_y.astype(jnp.float32)).astype(jnp.bfloat16)
        return jnp.einsum('pzxy,pqzw->qwxy', half_image.astype(jnp.float32), table_z.astype(jnp.float32)).astype(jnp.bfloat16)

    def coil_step(running, coil_id):
        comb_sum, back_sum = running
        spectrum = lax.dynamic_index_in_dim(k_space, coil_id, 1, keepdims=False) * sampled[None, :, None, :]
        cot_coil = lax.dynamic_index_in_dim(cotangent, coil_id, 1, keepdims=False)
        sens_f = lax.dynamic_index_in_dim(sens_maps, coil_id, 1, keepdims=False).astype(jnp.float32)
        coil_image = inverse_volume(spectrum)
        back_image = inverse_volume(cot_coil)
        image_f = coil_image.astype(jnp.float32)
        back_f = back_image.astype(jnp.float32)
        comb_sum = comb_sum + jnp.stack([sens_f[0] * image_f[0] + sens_f[1] * image_f[1], sens_f[0] * image_f[1] - sens_f[1] * image_f[0]])
        back_sum = back_sum - jnp.stack([sens_f[0] * back_f[0] + sens_f[1] * back_f[1], sens_f[0] * back_f[1] - sens_f[1] * back_f[0]])
        return ((comb_sum, back_sum), (coil_image, back_image))
    zeros_f = jnp.zeros((2, NZ, NX, NY), jnp.float32)
    (comb_sum, back_sum), (images, back_images) = lax.scan(coil_step, (zeros_f, zeros_f), jnp.arange(C, dtype=jnp.int32))
    combined = comb_sum.astype(jnp.bfloat16)
    grad_reg = back_sum.astype(jnp.bfloat16)
    block_depth = 16
    blocks = NZ // block_depth

    def to_blocks(values):
        return jnp.moveaxis(values.reshape(values.shape[0], blocks, block_depth, NX, NY), 1, 0)

    def from_blocks(values):
        return jnp.moveaxis(values, 0, 1).reshape(values.shape[1], NZ, NX, NY)

    def extend(values):
        return jnp.pad(values, ((0, 0), (0, 0), (1, 1), (0, 0)))

    def one_block(block_pair):
        return regularize(block_pair[0], block_pair[1], w_first, b_first, w_second, b_second, extend)
    reg_blocks, comb_grad_blocks, grad_blocks = lax.map(one_block, (to_blocks(combined), to_blocks(grad_reg)))
    reg_f = from_blocks(reg_blocks).astype(jnp.float32)
    comb_grad_f = from_blocks(comb_grad_blocks).astype(jnp.float32)
    scaling = 1.0 / math.sqrt(NX * NY * NZ)
    grad_w1 = lax.optimization_barrier(jnp.sum(grad_blocks[0], axis=0)) * scaling
    grad_b1 = lax.optimization_barrier(jnp.sum(grad_blocks[1], axis=0)) * scaling
    grad_w2 = lax.optimization_barrier(jnp.sum(grad_blocks[2], axis=0)) * scaling
    grad_b2 = lax.optimization_barrier(jnp.sum(grad_blocks[3], axis=0)) * scaling

    def sens_grad(coil_id):
        image_f = images[coil_id].astype(jnp.float32)
        back_f = back_images[coil_id].astype(jnp.float32)
        real_part = -(back_f[0] * reg_f[0] + back_f[1] * reg_f[1]) + image_f[0] * comb_grad_f[0] + image_f[1] * comb_grad_f[1]
        imag_part = -(back_f[1] * reg_f[0] - back_f[0] * reg_f[1]) + image_f[1] * comb_grad_f[0] - image_f[0] * comb_grad_f[1]
        return jnp.stack([real_part, imag_part]).astype(jnp.bfloat16)
    grad_sens = jnp.moveaxis(lax.map(sens_grad, jnp.arange(C, dtype=jnp.int32)), 0, 1)
    return (grad_sens, grad_w1, grad_b1, grad_w2, grad_b2)
```

```python
import math

import jax
import jax.numpy as jnp
import numpy as np
import ml_dtypes
from jax import lax
from jax.experimental import pallas as pl
from jax.experimental.pallas import tpu as pltpu
from jax.sharding import PartitionSpec as P

MESH = pl.DeviceIdType.MESH
BF = jnp.bfloat16
F32 = jnp.float32
NS, NCOIL = 64, 4
NY, NZ, CH, LINES = 320, 256, 18, 40
CL, ZL = 4, 4
BLK, NB = 32, 5
HV, HU, US = 34, 36, 40
MR, KR = 640, 256
PR = 176
TR = 192
LN = NB * 128


def one_hot(rows, cols, pairs):
    table = np.zeros((rows, cols), np.float32)
    for r, c in pairs:
        table[r, c] = 1.0
    return table


def dft_matrix(length):
    position = np.arange(length)
    angles = 2.0 * math.pi / length * ((position[:, None] * position[None, :]) % length)
    cosine = np.cos(angles) / math.sqrt(length)
    sine = np.sin(angles) / math.sqrt(length)
    return np.block([[cosine, sine], [-sine, cosine]]).astype(ml_dtypes.bfloat16)


def make_constants():
    bf = ml_dtypes.bfloat16
    hid = [(ch * HV + v, ch, v) for ch in range(CH) for v in range(HV)]
    inp = [((i * 3 + a) * US + u, i, a, u) for i in range(2) for a in range(3) for u in range(HU)]
    spread = one_hot(MR, 128, [(r, ch) for r, ch, _ in hid])
    pick1 = np.stack(
        [one_hot(128, KR, [(i * 9 + a * 3 + b, r) for r, i, a, _ in inp]) for b in range(3)]
    )
    pick2 = np.stack(
        [
            one_hot(128, KR, [(i * 9 + (2 - a) * 3 + (2 - b), r) for r, i, a, _ in inp])
            for b in range(3)
        ]
    )
    rowpick = np.stack(
        [
            one_hot(
                64, 128, [(q * BLK + t, q * 9 + a * 3 + b) for q in range(2) for t in range(BLK)]
            )
            for a in range(3)
            for b in range(3)
        ]
    )
    gap1 = np.full((MR, KR), 99.0, np.float32)
    for r, _, v in hid:
        for s, _, _, u in inp:
            gap1[r, s] = u - v
    gap2 = np.full((64, MR), 99.0, np.float32)
    for q in range(2):
        for t in range(BLK):
            for r, _, v in hid:
                gap2[q * BLK + t, r] = v - t
    inner = np.zeros((MR,), bool)
    for r, _, v in hid:
        inner[r] = 1 <= v <= BLK
    gap3 = np.where(inner[None, :], gap1.T, 99.0).astype(np.float32)
    sel_a = spread
    sel_b = np.roll(spread, 32, axis=1)
    middle = np.broadcast_to(inner[None, :], (8, MR)).astype(np.float32)
    edge = np.zeros((MR, 128), np.float32)
    for r, _, v in hid:
        edge[r] = 1.0 if v == 0 else 2.0 if v == HV - 1 else 0.0
    return [
        dft_matrix(NY),
        dft_matrix(NZ),
        spread.astype(bf),
        np.ascontiguousarray(spread.T).astype(bf),
        pick1.astype(bf),
        pick2.astype(bf),
        rowpick.astype(bf),
        gap1,
        gap2,
        gap3,
        sel_a,
        sel_b,
        middle,
        edge,
    ]


def mm(a, b):
    return jnp.dot(a, b, preferred_element_type=F32)


def mm_nt(a, b):
    return lax.dot_general(a, b, (((1,), (1,)), ((), ())), preferred_element_type=F32)


def cascade_kernel(*refs):
    n_const = 14
    k_hbm, cot_hbm, sens_hbm, lines_ref, lines2_ref, w1m_ref, w2m_ref, b1_ref, b2_ref = refs[:9]
    const_hbm = refs[9 : 9 + n_const]
    out_ref, gw_ref = refs[9 + n_const : 11 + n_const]
    rest = refs[11 + n_const :]
    consts = rest[:n_const]
    (
        kv, cv, sv, ksc, ksend, krecv, csc, csend, crecv, pos, ex, hsc, ht,
        img, part, rsrecv, hrecv, tmp, vbuf, hid, act, gp, bcol,
        w1b, w2f, w2b, w1f, agsend, agrecv, rows_a, rows_b, ar1, ar2, ar3,
        ld_sem, c_ld, k_s, k_r, c_s, c_r, rs_s, rs_r, h_s, h_r, ag_s, ag_r, ar_s, ar_r,
    ) = rest[n_const:]
    (ty, tz, spread, spread_t, pick1, pick2, rowpick, gap1, gap2, gap3, sel_a, sel_b, middle, edge) = consts

    me = lax.axis_index("space")
    co = lax.axis_index("coil")
    hz = co // 2
    hy = co % 2

    barrier = pltpu.get_barrier_semaphore()

    def greet(j, _):
        pl.semaphore_signal(
            barrier, inc=1, device_id=(lax.rem(me + j, NS), co), device_id_type=MESH
        )
        return 0

    lax.fori_loop(1, NS, greet, 0)
    for j in range(1, NCOIL):
        pl.semaphore_signal(
            barrier, inc=1, device_id=(me, lax.rem(co + j, NCOIL)), device_id_type=MESH
        )
    load_k = pltpu.make_async_copy(k_hbm, kv, ld_sem.at[0])
    load_c = pltpu.make_async_copy(cot_hbm, cv, ld_sem.at[1])
    load_s = pltpu.make_async_copy(sens_hbm, sv, ld_sem.at[2])
    load_k.start()
    load_c.start()
    loads = [
        pltpu.make_async_copy(src, dst, c_ld.at[n])
        for n, (src, dst) in enumerate(zip(const_hbm, consts))
    ]
    for load in loads:
        load.start()
    load_s.start()

    load_k.wait()
    y_rows = lax.broadcasted_iota(jnp.int32, (NY, 128), 0)

    def hot(z):
        row = lines2_ref[pl.ds(me * ZL + z, 1), :]
        return jnp.where(y_rows == row, 1.0, 0.0).astype(BF)

    hots = [hot(z) for z in range(ZL)]
    for p in range(2):
        for zlo in range(2):
            packed = mm(kv[p, :, zlo].reshape(CL * NS, NY), hots[zlo])
            packed += mm(kv[p, :, zlo + 2].reshape(CL * NS, NY), hots[zlo + 2])
            ksc[pl.ds((p * 2 + zlo) * 256, 256), :] = packed

    def pack_k(x, _):
        ksend[x] = ksc[pl.ds(x, 16, stride=NS), :].astype(BF)
        return 0

    lax.fori_loop(0, NS, pack_k, 0, unroll=4)

    pl.semaphore_wait(barrier, NS - 1 + NCOIL - 1)

    def spread_out(src, dst, s_sem, r_sem):
        pltpu.make_async_copy(src.at[me], dst.at[me], r_sem).start()

        def send(j, _):
            to = lax.rem(me + j, NS)
            pltpu.make_async_remote_copy(
                src_ref=src.at[to],
                dst_ref=dst.at[me],
                send_sem=s_sem,
                recv_sem=r_sem,
                device_id=(to, co),
                device_id_type=MESH,
            ).start()
            return 0

        lax.fori_loop(1, NS, send, 0)

    spread_out(ksend, krecv, k_s, k_r)

    load_c.wait()
    loads[0].wait()

    def cot_y(zl, _):
        rows = mm(cv[0, :, zl].reshape(CL * NS, NY), ty[0:NY])
        rows += mm(cv[1, :, zl].reshape(CL * NS, NY), ty[NY:])
        for j in range(5):
            csc[j, pl.ds(pl.multiple_of(zl * 256, 256), 256), :] = rows[:, j * 128 : (j + 1) * 128]
        return 0

    lax.fori_loop(0, ZL, cot_y, 0)

    def pack_c(x, _):
        for j in range(5):
            lanes = slice(j * 128, (j + 1) * 128)
            csend[x, :, lanes] = csc[j, pl.ds(x, 16, stride=NS), :].astype(BF)
        return 0

    lax.fori_loop(0, NS, pack_c, 0, unroll=2)
    spread_out(csend, crecv, c_s, c_r)

    for load in loads[1:]:
        load.wait()
    lane_y = lax.broadcasted_iota(jnp.int32, (32, MR), 1)
    lane_y = jnp.where(lane_y >= NY, lane_y - NY, lane_y)
    upper = jnp.where(lax.broadcasted_iota(jnp.int32, (32, MR), 0) % 4 >= 2, 64, 0)

    def find(g, _):
        rows = pl.ds(pl.multiple_of(g * 32, 32), 32)
        lines = lines_ref[rows, :]
        place = jnp.full((32, MR), 127, jnp.int32)
        for line in range(LINES):
            place = jnp.where(lines[:, line : line + 1] == lane_y, upper + line, place)
        pos[rows, :] = place
        return 0

    lax.fori_loop(0, NZ // 32, find, 0)

    w1 = w1m_ref[...]
    w2 = w2m_ref[...]
    sp = spread[...]
    spt = spread_t[...]
    by_hidden1 = mm(sp, w1).astype(BF)
    by_hidden2 = mm(sp, w2).astype(BF)
    band1 = jnp.zeros((MR, KR), F32)
    band2 = jnp.zeros((MR, KR), F32)
    for b in range(3):
        hit = gap1[...] == float(b)
        band1 += jnp.where(hit, mm(by_hidden1, pick1[b]), 0.0)
        band2 += jnp.where(hit, mm(by_hidden2, pick2[b]), 0.0)
    w1b[...] = band1.astype(BF)
    w2f[...] = band2.astype(BF)
    for a in range(3):
        out2 = jnp.zeros((64, MR), F32)
        out1 = jnp.zeros((64, MR), F32)
        for b in range(3):
            hit = gap2[...] == float(b)
            out2 += jnp.where(hit, mm(mm_nt(rowpick[a * 3 + b], w2).astype(BF), spt), 0.0)
            flipped = rowpick[(2 - a) * 3 + (2 - b)]
            out1 += jnp.where(hit, mm(mm_nt(flipped, w1).astype(BF), spt), 0.0)
        w2b[a] = out2.astype(BF)
        w1f[a] = out1.astype(BF)
    bias = jnp.sum(sp.astype(F32) * b1_ref[...], axis=1, keepdims=True)
    bcol[...] = jnp.broadcast_to(bias, (MR, 128))
    zero_rows = jnp.zeros((KR - 6 * US, 3 * LN), BF)
    for n in range(2):
        vbuf[n, 6 * US :, :] = zero_rows
    for j in range(5):
        for i in range(2):
            tmp[j, i, 0:8, :] = jnp.zeros((8, 128), F32)
            tmp[j, i, 176:TR, :] = jnp.zeros((TR - 176, 128), F32)
    load_s.wait()

    def to_image(n):
        def one_coil(c, _):
            for j in range(5):
                block = hsc[j, pl.ds(c, NZ, stride=CL), :]
                ht[j * 128 : (j + 1) * 128, :] = block.T.astype(BF)
            both = jnp.concatenate([ht[0:NY, :], ht[NY:, :]], axis=1)
            img[n, c] = mm(both, tz[...]).astype(BF)
            return 0

        lax.fori_loop(0, CL, one_coil, 0)

        def combine(g, _):
            rows = pl.ds(pl.multiple_of(g * 16, 16), 16)
            re = jnp.zeros((16, NZ), F32)
            im = jnp.zeros((16, NZ), F32)
            for c in range(CL):
                both = img[n, c, rows, :].astype(F32)
                i0, i1 = both[:, :NZ], both[:, NZ:]
                s0 = sv[0, c, rows, :].astype(F32)
                s1 = sv[1, c, rows, :].astype(F32)
                re += s0 * i0 + s1 * i1
                im += s0 * i1 - s1 * i0
            if n == 1:
                re, im = -re, -im
            part[n, 0, rows, :] = re.astype(BF)
            part[n, 1, rows, :] = im.astype(BF)
            return 0

        lax.fori_loop(0, NY // 16, combine, 0)

    def piece(n, to):
        return part.at[
            n,
            :,
            pl.ds(pl.multiple_of((to % 2) * 144, 16), PR),
            pl.ds(pl.multiple_of((to // 2) * 128, 128), 128),
        ]

    def coil_send(n):
        pltpu.make_async_copy(piece(n, co), rsrecv.at[n, co], rs_r.at[n]).start()
        for j in range(1, NCOIL):
            to = lax.rem(co + j, NCOIL)
            pltpu.make_async_remote_copy(
                src_ref=piece(n, to),
                dst_ref=rsrecv.at[n, co],
                send_sem=rs_s.at[n],
                recv_sem=rs_r.at[n],
                device_id=(me, to),
                device_id_type=MESH,
            ).start()

    def coil_sum(n):
        pltpu.make_async_copy(rsrecv.at[n], rsrecv.at[n], rs_r.at[n]).wait()
        for q in range(2):
            total = rsrecv[n, 0, q].astype(F32)
            for j in range(1, NCOIL):
                total += rsrecv[n, j, q].astype(F32)
            hrecv[n, 4, q] = total.astype(BF)
        for slot, off in enumerate((-2, -1, 1, 2)):
            to = lax.rem(me + off + NS, NS)
            pltpu.make_async_remote_copy(
                src_ref=hrecv.at[n, 4],
                dst_ref=hrecv.at[n, 3 - slot],
                send_sem=h_s.at[n],
                recv_sem=h_r.at[n],
                device_id=(to, co),
                device_id_type=MESH,
            ).start()

    def windows(n):
        pltpu.make_async_copy(hrecv.at[n, pl.ds(0, 4)], hrecv.at[n, pl.ds(0, 4)], h_r.at[n]).wait()
        for j, slot in enumerate((0, 1, 4, 2, 3)):
            x = me + j - 2
            inside = jnp.logical_and(x >= 0, x < NS)
            for q in range(2):
                got = hrecv[n, slot, q].astype(F32)
                tmp[j, q, 2 : 2 + PR, :] = jnp.where(inside, got, 0.0)
        for x3 in range(3):
            for blk in range(NB):
                lanes = slice((x3 * NB + blk) * 128, (x3 * NB + blk + 1) * 128)
                rows = pl.ds(pl.multiple_of(hy * 16, 16) + blk * BLK, US)
                column = [tmp[x3 + a, q, rows, :] for q in range(2) for a in range(3)]
                vbuf[n, 0 : 6 * US, lanes] = jnp.concatenate(column, axis=0).astype(BF)

    def into_hidden(n, w):
        for x3 in range(3):
            lanes = slice(x3 * LN, (x3 + 1) * LN)
            hid[n, :, lanes] = mm(w[...], vbuf[n, :, lanes])

    x_ok = [jnp.logical_and(me + d >= 0, me + d < NS) for d in (-1, 0, 1)]

    def keep(value, kind, x3, blk):
        if blk == 0:
            value = jnp.where(jnp.logical_and(kind == 1.0, hy == 0), 0.0, value)
        if blk == NB - 1:
            value = jnp.where(jnp.logical_and(kind == 2.0, hy == 1), 0.0, value)
        if x3 != 1:
            value = jnp.where(x_ok[x3], value, 0.0)
        return value

    def out_of_hidden(values, w):
        total = mm(w[0], values[:, 0:LN])
        total += mm(w[1], values[:, LN : 2 * LN])
        total += mm(w[2], values[:, 2 * LN :])
        return total

    def gather_send(n):
        pltpu.make_async_copy(agsend.at[n], agrecv.at[n, co], ag_r.at[n]).start()
        for j in range(1, NCOIL):
            to = lax.rem(co + j, NCOIL)
            pltpu.make_async_remote_copy(
                src_ref=agsend.at[n],
                dst_ref=agrecv.at[n, co],
                send_sem=ag_s.at[n],
                recv_sem=ag_r.at[n],
                device_id=(me, to),
                device_id_type=MESH,
            ).start()

    pltpu.make_async_copy(krecv, krecv, k_r).wait()
    low_rows = lax.broadcasted_iota(jnp.int32, (8, MR), 0) < 4
    low_lanes = lax.broadcasted_iota(jnp.int32, (8, 128), 1) < 64

    def pick(values, index):
        return jnp.take_along_axis(values, index, axis=1, mode="promise_in_bounds")

    def expand(s, _):
        got = krecv[s].astype(F32)
        halves = []
        for zhi in range(2):
            first = pos[pl.ds(s * 4 + 2 * zhi, 1), :]
            second = pos[pl.ds(s * 4 + 2 * zhi + 1, 1), :]
            index = jnp.where(
                low_rows,
                jnp.broadcast_to(first, (8, MR)),
                jnp.broadcast_to(second, (8, MR)),
            )
            at = [index[:, j * 128 : (j + 1) * 128] for j in range(5)]
            re, im = got[0:8], got[8:16]
            halves.append(
                jnp.concatenate(
                    [
                        pick(re, at[0]),
                        pick(re, at[1]),
                        jnp.where(low_lanes, pick(re, at[2]), pick(im, at[2])),
                        pick(im, at[3]),
                        pick(im, at[4]),
                    ],
                    axis=1,
                )
            )
        ex[pl.ds(pl.multiple_of(s * 16, 16), 16), :] = jnp.concatenate(halves, axis=0).astype(BF)
        return 0

    lax.fori_loop(0, NS, expand, 0, unroll=2)

    def k_y(g, _):
        rows = pl.ds(pl.multiple_of(g * 256, 256), 256)
        half = mm(ex[rows, :], ty[...]).astype(BF).astype(F32)
        for j in range(5):
            hsc[j, rows, :] = half[:, j * 128 : (j + 1) * 128]
        return 0

    lax.fori_loop(0, 4, k_y, 0)
    to_image(0)
    coil_send(0)
    coil_sum(0)
    windows(0)
    into_hidden(0, w1b)

    def activate(g, _):
        rows = pl.ds(pl.multiple_of(g * 16, 16), 16)
        kind = edge[rows, :]
        add = bcol[rows, :]
        for x3 in range(3):
            for blk in range(NB):
                lanes = slice((x3 * NB + blk) * 128, (x3 * NB + blk + 1) * 128)
                h = hid[0, rows, lanes] + add
                s = 0.5 * jnp.tanh(0.5 * h) + 0.5
                act[rows, lanes] = keep(h * s, kind, x3, blk).astype(BF)
                hid[0, rows, lanes] = s * (1.0 + h * (1.0 - s))
        return 0

    lax.fori_loop(0, MR // 16, activate, 0)
    regularized = out_of_hidden(act, w2b)
    for q in range(2):
        for blk in range(NB):
            block = regularized[q * BLK : (q + 1) * BLK, blk * 128 : (blk + 1) * 128] + b2_ref[q]
            agsend[0, q, blk * BLK : (blk + 1) * BLK, :] = block.astype(BF)
    gather_send(0)

    pltpu.make_async_copy(crecv, crecv, c_r).wait()

    def widen(s, _):
        got = crecv[s].astype(F32)
        for j in range(5):
            hsc[j, pl.ds(pl.multiple_of(s * 16, 16), 16), :] = got[:, j * 128 : (j + 1) * 128]
        return 0

    lax.fori_loop(0, NS, widen, 0, unroll=4)
    to_image(1)
    coil_send(1)
    coil_sum(1)
    windows(1)
    into_hidden(1, w2f)

    def grad_hidden(g, _):
        rows = pl.ds(pl.multiple_of(g * 16, 16), 16)
        kind = edge[rows, :]
        for x3 in range(3):
            for blk in range(NB):
                lanes = slice((x3 * NB + blk) * 128, (x3 * NB + blk + 1) * 128)
                value = hid[1, rows, lanes] * hid[0, rows, lanes]
                gp[rows, lanes] = keep(value, kind, x3, blk).astype(BF)
        return 0

    lax.fori_loop(0, MR // 16, grad_hidden, 0)
    grad_comb = out_of_hidden(gp, w1f)
    for q in range(2):
        for blk in range(NB):
            block = grad_comb[q * BLK : (q + 1) * BLK, blk * 128 : (blk + 1) * 128]
            agsend[1, q, blk * BLK : (blk + 1) * BLK, :] = block.astype(BF)
    gather_send(1)

    rows_a[...] = jnp.zeros((24, MR), F32)
    rows_b[...] = jnp.zeros((24, MR), F32)
    gp_mid = gp[:, LN : 2 * LN]
    cross = mm_nt(vbuf[0, :, LN : 2 * LN], gp_mid)
    for i in range(2):
        for a in range(3):
            rows = slice((i * 3 + a) * US, (i * 3 + a + 1) * US)
            block = cross[rows, :]
            gap = gap3[rows, :]
            for b in range(3):
                at = i * 9 + a * 3 + b
                rows_a[at : at + 1, :] = jnp.sum(
                    jnp.where(gap == float(b), block, 0.0), axis=0, keepdims=True
                )
    sums = mm_nt(jnp.ones((8, LN), BF), gp_mid) * middle[...]
    rows_a[18:19, :] = sums[0:1, :]
    own = jnp.concatenate(
        [
            jnp.concatenate(
                [
                    hrecv[1, 4, q, pl.ds(pl.multiple_of(hy * 16, 16) + blk * BLK, BLK), :]
                    for blk in range(NB)
                ],
                axis=1,
            )
            for q in range(2)
        ],
        axis=0,
    )
    for a in range(3):
        cross = mm_nt(own, act[:, a * LN : (a + 1) * LN])
        for q in range(2):
            rows = slice(q * BLK, (q + 1) * BLK)
            for b in range(3):
                at = a * 6 + b * 2 + q
                rows_b[at : at + 1, :] = jnp.sum(
                    jnp.where(gap2[rows, :] == float(b), cross[rows, :], 0.0),
                    axis=0,
                    keepdims=True,
                )
    high = lax.Precision.HIGHEST
    grads = jnp.dot(rows_a[...], sel_a[...], precision=high, preferred_element_type=F32)
    grads += jnp.dot(rows_b[...], sel_b[...], precision=high, preferred_element_type=F32)
    at_row = lax.broadcasted_iota(jnp.int32, (24, 128), 0)
    at_lane = lax.broadcasted_iota(jnp.int32, (24, 128), 1)
    own_f = own.astype(F32)
    for q in range(2):
        spot = jnp.logical_and(at_row == 18, at_lane == 32 + q)
        grads += jnp.where(spot, jnp.sum(own_f[q * BLK : (q + 1) * BLK]), 0.0)

    def share(n, buf, count, mine, device):
        buf[mine] = grads_in[n]
        for j in range(1, count):
            to = lax.rem(mine + j, count)
            pltpu.make_async_remote_copy(
                src_ref=buf.at[mine],
                dst_ref=buf.at[mine],
                send_sem=ar_s.at[n],
                recv_sem=ar_r.at[n],
                device_id=device(to),
                device_id_type=MESH,
            ).start()

    def collect(n, buf, count):
        rest_of = buf.at[pl.ds(0, count - 1)]
        pltpu.make_async_copy(rest_of, rest_of, ar_r.at[n]).wait()
        total = buf[0]
        for j in range(1, count):
            total += buf[j]
        return total

    row_y, row_zc = me // 16, me % 16
    grads_in = [grads]
    share(0, ar1, 16, row_zc, lambda to: (row_y * 16 + to, co))

    pltpu.make_async_copy(agrecv.at[0], agrecv.at[0], ag_r.at[0]).wait()
    pltpu.make_async_copy(agrecv.at[1], agrecv.at[1], ag_r.at[1]).wait()

    def finish(g, _):
        for half_y in range(2):
            for half_z in range(2):
                slot = half_z * 2 + half_y
                src = pl.ds(pl.multiple_of(g * 16, 16), 16)
                dst = pl.ds(pl.multiple_of(half_y * 160 + g * 16, 16), 16)
                lo = slice(half_z * 128, half_z * 128 + 128)
                hi = slice(NZ + half_z * 128, NZ + half_z * 128 + 128)
                r0 = agrecv[0, slot, 0, src, :].astype(F32)
                r1 = agrecv[0, slot, 1, src, :].astype(F32)
                g0 = agrecv[1, slot, 0, src, :].astype(F32)
                g1 = agrecv[1, slot, 1, src, :].astype(F32)
                for c in range(CL):
                    i0 = img[0, c, dst, lo].astype(F32)
                    i1 = img[0, c, dst, hi].astype(F32)
                    k0 = img[1, c, dst, lo].astype(F32)
                    k1 = img[1, c, dst, hi].astype(F32)
                    re = -(k0 * r0 + k1 * r1) + i0 * g0 + i1 * g1
                    im = -(k1 * r0 - k0 * r1) + i1 * g0 - i0 * g1
                    out_ref[0, c, dst, lo] = re.astype(BF)
                    out_ref[1, c, dst, lo] = im.astype(BF)
        return 0

    lax.fori_loop(0, 10, finish, 0)

    grads_in.append(collect(0, ar1, 16))
    share(1, ar2, 4, row_y, lambda to: (to * 16 + row_zc, co))
    grads_in.append(collect(1, ar2, 4))
    share(2, ar3, 4, co, lambda to: (me, to))
    gw_ref[...] = collect(2, ar3, 4) * (1.0 / math.sqrt(NS * NY * NZ))

    def sent(ref, sem):
        pltpu.make_async_copy(ref, ref, sem).wait()

    sent(ksend.at[pl.ds(0, NS - 1)], k_s)
    sent(csend.at[pl.ds(0, NS - 1)], c_s)
    for n in range(2):
        sent(rsrecv.at[n, pl.ds(0, NCOIL - 1)], rs_s.at[n])
        sent(hrecv.at[n, pl.ds(0, 4)], h_s.at[n])
        sent(agrecv.at[n, pl.ds(0, NCOIL - 1)], ag_s.at[n])
    sent(ar1.at[pl.ds(0, 15)], ar_s.at[0])
    sent(ar2.at[pl.ds(0, 3)], ar_s.at[1])
    sent(ar3.at[pl.ds(0, 3)], ar_s.at[2])


def on_device(k_space, cotangent, sens_maps, line_index, w_first, b_first, w_second, b_second):
    constants = make_constants()
    sens = jnp.transpose(sens_maps.reshape(2, CL, NZ, NY), (0, 1, 3, 2))
    lines = jnp.pad(line_index, ((0, 0), (0, 128 - LINES)), constant_values=-1)
    upper = (jnp.arange(NZ) % 4 >= 2)[:, None]
    lines2 = jnp.where(upper, jnp.roll(lines, 64, axis=1), lines)
    w1m = jnp.pad(w_first.reshape(CH, 18), ((0, 128 - CH), (0, 110)))
    w2m = jnp.pad(jnp.transpose(w_second, (1, 0, 2, 3)).reshape(CH, 18), ((0, 128 - CH), (0, 110)))
    b1 = jnp.pad(b_first, (0, 110)).reshape(1, 128)
    vm = pl.BlockSpec(memory_space=pltpu.VMEM)
    anym = pl.BlockSpec(memory_space=pl.ANY)
    dma = pltpu.SemaphoreType.DMA
    scratch = [pltpu.VMEM(c.shape, c.dtype) for c in constants]
    scratch += [
        pltpu.VMEM((2, CL, ZL, NS, NY), BF),
        pltpu.VMEM((2, CL, ZL, NS, NY), BF),
        pltpu.VMEM((2, CL, NY, NZ), BF),
        pltpu.VMEM((16 * NS, 128), F32),
        pltpu.VMEM((NS, 16, 128), BF),
        pltpu.VMEM((NS, 16, 128), BF),
        pltpu.VMEM((5, 16 * NS, 128), F32),
        pltpu.VMEM((NS, 16, 640), BF),
        pltpu.VMEM((NS, 16, 640), BF),
        pltpu.VMEM((NZ, 640), jnp.int32),
        pltpu.VMEM((NZ * CL, 640), BF),
        pltpu.VMEM((5, NZ * CL, 128), F32),
        pltpu.VMEM((640, NZ), BF),
        pltpu.VMEM((2, CL, NY, 2 * NZ), BF),
        pltpu.VMEM((2, 2, NY, NZ), BF),
        pltpu.VMEM((2, NCOIL, 2, PR, 128), BF),
        pltpu.VMEM((2, 5, 2, PR, 128), BF),
        pltpu.VMEM((5, 2, TR, 128), F32),
        pltpu.VMEM((2, KR, 3 * LN), BF),
        pltpu.VMEM((2, MR, 3 * LN), F32),
        pltpu.VMEM((MR, 3 * LN), BF),
        pltpu.VMEM((MR, 3 * LN), BF),
        pltpu.VMEM((MR, 128), F32),
        pltpu.VMEM((MR, KR), BF),
        pltpu.VMEM((MR, KR), BF),
        pltpu.VMEM((3, 64, MR), BF),
        pltpu.VMEM((3, 64, MR), BF),
        pltpu.VMEM((2, 2, NY // 2, 128), BF),
        pltpu.VMEM((2, NCOIL, 2, NY // 2, 128), BF),
        pltpu.VMEM((24, MR), F32),
        pltpu.VMEM((24, MR), F32),
        pltpu.VMEM((16, 24, 128), F32),
        pltpu.VMEM((4, 24, 128), F32),
        pltpu.VMEM((4, 24, 128), F32),
        dma((3,)),
        dma((len(constants),)),
        dma,
        dma,
        dma,
        dma,
        dma((2,)),
        dma((2,)),
        dma((2,)),
        dma((2,)),
        dma((2,)),
        dma((2,)),
        dma((3,)),
        dma((3,)),
    ]
    grad_sens, grads = pl.pallas_call(
        cascade_kernel,
        out_shape=(
            jax.ShapeDtypeStruct((2, CL, NY, NZ), BF),
            jax.ShapeDtypeStruct((24, 128), F32),
        ),
        in_specs=[anym] * 3
        + [vm] * 5
        + [pl.BlockSpec(memory_space=pltpu.SMEM)]
        + [anym] * len(constants),
        out_specs=(vm, vm),
        scratch_shapes=scratch,
        compiler_params=pltpu.CompilerParams(
            collective_id=0, has_side_effects=True, vmem_limit_bytes=60 * 1024 * 1024
        ),
    )(k_space, cotangent, sens, lines, lines2, w1m, w2m, b1, b_second, *constants)
    grad_sens = jnp.transpose(grad_sens, (0, 1, 3, 2)).reshape(2, CL, NZ, 1, NY)
    grad_w1 = jnp.transpose(grads[0:18, 0:CH]).reshape(CH, 2, 3, 3)
    grad_b1 = grads[18, 0:CH]
    grad_w2 = jnp.transpose(grads[0:18, 32 : 32 + CH].reshape(3, 3, 2, CH), (2, 3, 0, 1))
    grad_b2 = grads[18, 32:34]
    return (grad_sens, grad_w1, grad_b1, grad_w2, grad_b2)


def solution(mesh):
    placed = (
        P(None, "coil", "space", None, None),
        P(None, "coil", "space", None, None),
        P(None, "coil", None, "space", None),
        P(),
        P(),
        P(),
        P(),
        P(),
    )
    return jax.shard_map(
        on_device,
        mesh=mesh,
        in_specs=placed,
        out_specs=(P(None, "coil", None, "space", None), P(), P(), P(), P()),
        check_vma=False,
    )
```

```python
import math

import jax
import jax.numpy as jnp
import numpy as np
import ml_dtypes
from jax import lax
from jax.experimental import pallas as pl
from jax.experimental.pallas import tpu as pltpu
from jax.sharding import PartitionSpec as P

MESH = pl.DeviceIdType.MESH
BF = jnp.bfloat16
F32 = jnp.float32
NS, NCOIL = 64, 4
NY, NZ, CH, LINES = 320, 256, 18, 40
CL, ZL = 4, 4
BLK, NB = 32, 5
HV, HU, US = 34, 36, 40
MR, KR = 640, 256
PR = 176
TR = 192
LN = NB * 128
NCH = 5
GROUPS = ((0, 2), (2, 4), (4, 5))
PIECES = (
    (0, 0, 0, 64, 0),
    (1, 0, 64, 48, 0),
    (1, 0, 112, 16, 1),
    (2, 0, 128, 48, 1),
    (2, 1, 144, 48, 0),
    (3, 1, 192, 64, 0),
    (4, 1, 256, 64, 1),
)
STEPS = ((0, 112), (112, 64))


def one_hot(rows, cols, pairs):
    table = np.zeros((rows, cols), np.float32)
    for r, c in pairs:
        table[r, c] = 1.0
    return table


def dft_matrix(length):
    position = np.arange(length)
    angles = 2.0 * math.pi / length * ((position[:, None] * position[None, :]) % length)
    cosine = np.cos(angles) / math.sqrt(length)
    sine = np.sin(angles) / math.sqrt(length)
    return np.block([[cosine, sine], [-sine, cosine]]).astype(ml_dtypes.bfloat16)


def make_constants():
    bf = ml_dtypes.bfloat16
    table_y = dft_matrix(NY).reshape(2 * NY, 2, NCH, 64)
    table_y = np.ascontiguousarray(table_y.transpose(0, 2, 1, 3)).reshape(2 * NY, 2 * NY)
    hid = [(ch * HV + v, ch, v) for ch in range(CH) for v in range(HV)]
    inp = [((i * 3 + a) * US + u, i, a, u) for i in range(2) for a in range(3) for u in range(HU)]
    spread = one_hot(MR, 128, [(r, ch) for r, ch, _ in hid])
    pick1 = np.stack(
        [one_hot(128, KR, [((a * 3 + b) * 2 + i, r) for r, i, a, _ in inp]) for b in range(3)]
    )
    pick2 = np.stack(
        [
            one_hot(128, KR, [((8 - a * 3 - b) * 2 + i, r) for r, i, a, _ in inp])
            for b in range(3)
        ]
    )
    rowpick = np.stack(
        [
            one_hot(
                64, 128, [(q * BLK + t, (a * 3 + b) * 2 + q) for q in range(2) for t in range(BLK)]
            )
            for a in range(3)
            for b in range(3)
        ]
    )
    gap1 = np.full((MR, KR), 99.0, np.float32)
    for r, _, v in hid:
        for s, _, _, u in inp:
            gap1[r, s] = u - v
    gap2 = np.full((64, MR), 99.0, np.float32)
    for q in range(2):
        for t in range(BLK):
            for r, _, v in hid:
                gap2[q * BLK + t, r] = v - t
    inner = np.zeros((MR,), bool)
    for r, _, v in hid:
        inner[r] = 1 <= v <= BLK
    gap3 = np.where(inner[None, :], gap1.T, 99.0).astype(np.float32)
    sel_a = spread
    sel_b = np.roll(spread, 32, axis=1)
    middle = np.broadcast_to(inner[None, :], (8, MR)).astype(np.float32)
    edge = np.zeros((MR, 128), np.float32)
    for r, _, v in hid:
        edge[r] = 1.0 if v == 0 else 2.0 if v == HV - 1 else 0.0
    return [
        table_y,
        dft_matrix(NZ),
        spread.astype(bf),
        np.ascontiguousarray(spread.T).astype(bf),
        pick1.astype(bf),
        pick2.astype(bf),
        rowpick.astype(bf),
        gap1,
        gap2,
        gap3,
        sel_a,
        sel_b,
        middle,
        edge,
    ]


def mm(a, b):
    return jnp.dot(a, b, preferred_element_type=F32)


def mm_nt(a, b):
    return lax.dot_general(a, b, (((1,), (1,)), ((), ())), preferred_element_type=F32)


def arrived(ref, sem):
    pltpu.make_async_copy(ref, ref, sem).wait()


def cascade_kernel(*refs):
    n_const = 14
    k_hbm, cot_hbm, sens_hbm, index_ref, first_ref, second_ref, b1_ref, b2_ref = refs[:8]
    const_hbm = refs[8 : 8 + n_const]
    pre_hbm, gw_ref = refs[8 + n_const : 10 + n_const]
    rest = refs[10 + n_const :]
    consts = rest[:n_const]
    (
        kv, cv, sv, ksc, ksend, krecv, csc, cs0, cs1, cs2, cr0, cr1, cr2, pos, ex, hsc,
        img, part, rsrecv, hrecv, tmp, vbuf, hid, act, gp, bcol,
        w1b, w2f, w2b, w1f, agsend, agrecv, regpart, outv, rows_a, rows_b, gsec, ar1, ar2, lines_ref, lines2_ref, wt,
        ld_sem, c_ld, o_sem, k_s, k_r, c_s, c_r, rs_s, rs_r, h_s, h_r, ag_s, ag_r, ar_s, ar_r,
    ) = rest[n_const:]
    (ty, tz, spread, spread_t, pick1, pick2, rowpick, gap1, gap2, gap3, sel_a, sel_b, middle, edge) = consts

    csend, crecv = (cs0, cs1, cs2), (cr0, cr1, cr2)
    me = lax.axis_index("space")
    co = lax.axis_index("coil")
    hz = co // 2
    hy = co % 2

    barrier = pltpu.get_barrier_semaphore()

    def greet(j, _):
        pl.semaphore_signal(
            barrier, inc=1, device_id=(lax.rem(me + j, NS), co), device_id_type=MESH
        )
        return 0

    lax.fori_loop(1, NS, greet, 0)
    for j in range(1, NCOIL):
        pl.semaphore_signal(
            barrier, inc=1, device_id=(me, lax.rem(co + j, NCOIL)), device_id_type=MESH
        )
    row_y, row_zc = me // 16, me % 16
    for jy in range(1, 4):
        for jc in range(1, NCOIL):
            there = (lax.rem(row_y + jy, 4) * 16 + row_zc, lax.rem(co + jc, NCOIL))
            pl.semaphore_signal(barrier, inc=1, device_id=there, device_id_type=MESH)
    load_k = pltpu.make_async_copy(k_hbm, kv, ld_sem.at[0])
    load_c = pltpu.make_async_copy(cot_hbm, cv, ld_sem.at[1])
    load_s = pltpu.make_async_copy(sens_hbm, sv, ld_sem.at[2])
    load_k.start()
    load_c.start()
    loads = [
        pltpu.make_async_copy(src, dst, c_ld.at[n])
        for n, (src, dst) in enumerate(zip(const_hbm, consts))
    ]
    for load in loads:
        load.start()
    load_s.start()

    turned = jnp.concatenate(
        [index_ref[...].astype(F32), jnp.full((128 - LINES, NZ), -1.0, F32)], axis=0
    )
    shifted = jnp.concatenate(
        [jnp.full((64, NZ), -1.0, F32), turned[0:64]], axis=0
    )
    late = lax.broadcasted_iota(jnp.int32, (128, NZ), 1) % 4 >= 2
    lines_ref[...] = turned.T.astype(jnp.int32)
    lines2_ref[...] = jnp.where(late, shifted, turned).T.astype(jnp.int32)
    load_k.wait()
    y_rows = lax.broadcasted_iota(jnp.int32, (NY, 128), 0)

    def hot(z):
        row = lines2_ref[pl.ds(me * ZL + z, 1), :]
        return jnp.where(y_rows == row, 1.0, 0.0).astype(BF)

    hots = [hot(z) for z in range(ZL)]
    for p in range(2):
        for zlo in range(2):
            packed = mm(kv[p, :, zlo].reshape(CL * NS, NY), hots[zlo])
            packed += mm(kv[p, :, zlo + 2].reshape(CL * NS, NY), hots[zlo + 2])
            ksc[pl.ds((p * 2 + zlo) * 256, 256), :] = packed

    def pack_k(x, _):
        ksend[x] = ksc[pl.ds(x, 16, stride=NS), :].astype(BF)
        return 0

    lax.fori_loop(0, NS, pack_k, 0, unroll=4)

    def spread_out(src, dst, s_sem, r_sem):
        pltpu.make_async_copy(src.at[me], dst.at[me], r_sem).start()

        def send(j, _):
            to = lax.rem(me + j, NS)
            pltpu.make_async_remote_copy(
                src_ref=src.at[to],
                dst_ref=dst.at[me],
                send_sem=s_sem,
                recv_sem=r_sem,
                device_id=(to, co),
                device_id_type=MESH,
            ).start()
            return 0

        lax.fori_loop(1, NS, send, 0)

    pl.semaphore_wait(barrier, NS - 1 + NCOIL - 1 + 9)
    spread_out(ksend, krecv, k_s, k_r)

    load_c.wait()
    loads[0].wait()

    def cot_y(zl, _):
        rows = mm(cv[0, :, zl].reshape(CL * NS, NY), ty[0:NY])
        rows += mm(cv[1, :, zl].reshape(CL * NS, NY), ty[NY:])
        for j in range(5):
            csc[j, pl.ds(pl.multiple_of(zl * 256, 256), 256), :] = rows[:, j * 128 : (j + 1) * 128]
        return 0

    lax.fori_loop(0, ZL, cot_y, 0)

    def pack_c(x, _):
        for n, (lo, hi) in enumerate(GROUPS):
            for j in range(lo, hi):
                lanes = slice((j - lo) * 128, (j - lo + 1) * 128)
                csend[n][x, :, lanes] = csc[j, pl.ds(x, 16, stride=NS), :].astype(BF)
        return 0

    lax.fori_loop(0, NS, pack_c, 0, unroll=2)

    for n in range(len(GROUPS)):
        spread_out(csend[n], crecv[n], c_s.at[n], c_r.at[n])

    for load in loads[1:]:
        load.wait()
    lane_y = lax.broadcasted_iota(jnp.int32, (32, MR), 1)
    lane_y = jnp.where(lane_y >= NY, lane_y - NY, lane_y)
    upper = jnp.where(lax.broadcasted_iota(jnp.int32, (32, MR), 0) % 4 >= 2, 64, 0)

    def find(g, _):
        rows = pl.ds(pl.multiple_of(g * 32, 32), 32)
        lines = lines_ref[rows, :]
        place = jnp.full((32, MR), 127, jnp.int32)
        for line in range(LINES):
            place = jnp.where(lines[:, line : line + 1] == lane_y, upper + line, place)
        pos[rows, :] = place
        return 0

    lax.fori_loop(0, NZ // 32, find, 0)

    wt[...] = jnp.zeros((2, 128, 128), F32)
    for n, ref in enumerate((first_ref, second_ref)):
        for a in range(3):
            for b in range(3):
                at = (a * 3 + b) * 2
                wt[n, at : at + 2, 0:CH] = ref[a, b].astype(F32)
    w1 = wt[0].astype(BF)
    w2 = wt[1].astype(BF)
    sp = spread[...]
    spt = spread_t[...]
    by_hidden1 = mm_nt(sp, w1).astype(BF)
    by_hidden2 = mm_nt(sp, w2).astype(BF)
    band1 = jnp.zeros((MR, KR), F32)
    band2 = jnp.zeros((MR, KR), F32)
    for b in range(3):
        hit = gap1[...] == float(b)
        band1 += jnp.where(hit, mm(by_hidden1, pick1[b]), 0.0)
        band2 += jnp.where(hit, mm(by_hidden2, pick2[b]), 0.0)
    w1b[...] = band1.astype(BF)
    w2f[...] = band2.astype(BF)
    for a in range(3):
        out2 = jnp.zeros((64, MR), F32)
        out1 = jnp.zeros((64, MR), F32)
        for b in range(3):
            hit = gap2[...] == float(b)
            out2 += jnp.where(hit, mm(mm(rowpick[a * 3 + b], w2).astype(BF), spt), 0.0)
            flipped = rowpick[(2 - a) * 3 + (2 - b)]
            out1 += jnp.where(hit, mm(mm(flipped, w1).astype(BF), spt), 0.0)
        w2b[a] = out2.astype(BF)
        w1f[a] = out1.astype(BF)
    lane = lax.broadcasted_iota(jnp.int32, (1, 128), 1)
    row = jnp.zeros((1, 128), F32)
    for ch in range(CH):
        row = jnp.where(lane == ch, b1_ref[ch], row)
    bias = jnp.sum(sp.astype(F32) * row, axis=1, keepdims=True)
    bcol[...] = jnp.broadcast_to(bias, (MR, 128))
    zero_rows = jnp.zeros((KR - 6 * US, 3 * LN), BF)
    for n in range(2):
        vbuf[n, 6 * US :, :] = zero_rows
    for j in range(5):
        for i in range(2):
            tmp[j, i, 0:8, :] = jnp.zeros((8, 128), F32)
            tmp[j, i, 176:TR, :] = jnp.zeros((TR - 176, 128), F32)
    load_s.wait()

    def to_image(n, j):
        columns = []
        for c in range(CL):
            block = hsc[j, pl.ds(c, NZ, stride=CL), :].T.astype(BF)
            columns.append(jnp.concatenate([block[0:64], block[64:128]], axis=1))
        image = mm(jnp.concatenate(columns, axis=0), tz[...]).astype(BF)
        for c in range(CL):
            img[n, c, j * 64 : (j + 1) * 64, :] = image[c * 64 : (c + 1) * 64]

        def combine(g, _):
            rows = pl.ds(pl.multiple_of(j * 64 + g * 16, 16), 16)
            re = jnp.zeros((16, NZ), F32)
            im = jnp.zeros((16, NZ), F32)
            for c in range(CL):
                both = img[n, c, rows, :].astype(F32)
                i0, i1 = both[:, :NZ], both[:, NZ:]
                s0 = sv[0, c, rows, :].astype(F32)
                s1 = sv[1, c, rows, :].astype(F32)
                re += s0 * i0 + s1 * i1
                im += s0 * i1 - s1 * i0
            if n == 1:
                re, im = -re, -im
            part[n, 0, rows, :] = re.astype(BF)
            part[n, 1, rows, :] = im.astype(BF)
            return 0

        lax.fori_loop(0, 4, combine, 0)

    def coil_send(n, chunk):
        for j, half, row, count, step in PIECES:
            if j != chunk:
                continue
            for half_z in range(2):
                to = half_z * 2 + half
                src = part.at[n, :, pl.ds(row, count), pl.ds(half_z * 128, 128)]
                dst = rsrecv.at[n, co, :, pl.ds(row - half * 144, count)]

                @pl.when(co == to)
                def _():
                    pltpu.make_async_copy(src, dst, rs_r.at[n, step]).start()

                @pl.when(co != to)
                def _():
                    pltpu.make_async_remote_copy(
                        src_ref=src,
                        dst_ref=dst,
                        send_sem=rs_s.at[n, step],
                        recv_sem=rs_r.at[n, step],
                        device_id=(me, to),
                        device_id_type=MESH,
                    ).start()

    def coil_sum(n, step):
        first, count = STEPS[step]
        rows = slice(first, first + count)
        arrived(rsrecv.at[n, :, :, pl.ds(first, count)], rs_r.at[n, step])
        for q in range(2):
            total = rsrecv[n, 0, q, rows].astype(F32)
            for j in range(1, NCOIL):
                total += rsrecv[n, j, q, rows].astype(F32)
            hrecv[n, 4, q, rows] = total.astype(BF)
        for slot, off in enumerate((-2, -1, 1, 2)):
            to = lax.rem(me + off + NS, NS)
            pltpu.make_async_remote_copy(
                src_ref=hrecv.at[n, 4, :, pl.ds(first, count)],
                dst_ref=hrecv.at[n, 3 - slot, :, pl.ds(first, count)],
                send_sem=h_s.at[n, step],
                recv_sem=h_r.at[n, step],
                device_id=(to, co),
                device_id_type=MESH,
            ).start()

    def windows(n):
        for step, (first, count) in enumerate(STEPS):
            arrived(hrecv.at[n, pl.ds(0, 4), :, pl.ds(first, count)], h_r.at[n, step])
        for j, slot in enumerate((0, 1, 4, 2, 3)):
            x = me + j - 2
            inside = jnp.logical_and(x >= 0, x < NS)
            for q in range(2):
                got = hrecv[n, slot, q].astype(F32)
                tmp[j, q, 2 : 2 + PR, :] = jnp.where(inside, got, 0.0)
        for x3 in range(3):
            for blk in range(NB):
                lanes = slice((x3 * NB + blk) * 128, (x3 * NB + blk + 1) * 128)
                rows = pl.ds(pl.multiple_of(hy * 16, 16) + blk * BLK, US)
                column = [tmp[x3 + a, q, rows, :] for q in range(2) for a in range(3)]
                vbuf[n, 0 : 6 * US, lanes] = jnp.concatenate(column, axis=0).astype(BF)

    def into_hidden(n, w):
        for x3 in range(3):
            lanes = slice(x3 * LN, (x3 + 1) * LN)
            hid[n, :, lanes] = mm(w[...], vbuf[n, :, lanes])

    x_ok = [jnp.logical_and(me + d >= 0, me + d < NS) for d in (-1, 0, 1)]

    def keep(value, kind, x3, blk):
        if blk == 0:
            value = jnp.where(jnp.logical_and(kind == 1.0, hy == 0), 0.0, value)
        if blk == NB - 1:
            value = jnp.where(jnp.logical_and(kind == 2.0, hy == 1), 0.0, value)
        if x3 != 1:
            value = jnp.where(x_ok[x3], value, 0.0)
        return value

    def out_of_hidden(values, w):
        total = mm(w[0], values[:, 0:LN])
        total += mm(w[1], values[:, LN : 2 * LN])
        total += mm(w[2], values[:, 2 * LN :])
        return total

    def gather_send(n):
        pltpu.make_async_copy(agsend.at[n], agrecv.at[n, co], ag_r.at[n]).start()
        for j in range(1, NCOIL):
            to = lax.rem(co + j, NCOIL)
            pltpu.make_async_remote_copy(
                src_ref=agsend.at[n],
                dst_ref=agrecv.at[n, co],
                send_sem=ag_s.at[n],
                recv_sem=ag_r.at[n],
                device_id=(me, to),
                device_id_type=MESH,
            ).start()

    def second_grad():
        rows_b[...] = jnp.zeros((24, MR), F32)
        own = jnp.concatenate(
            [
                jnp.concatenate(
                    [
                        hrecv[1, 4, q, pl.ds(pl.multiple_of(hy * 16, 16) + blk * BLK, BLK), :]
                        for blk in range(NB)
                    ],
                    axis=1,
                )
                for q in range(2)
            ],
            axis=0,
        )
        for a in range(3):
            cross = mm_nt(own, act[:, a * LN : (a + 1) * LN])
            for q in range(2):
                rows = slice(q * BLK, (q + 1) * BLK)
                for b in range(3):
                    at = a * 6 + b * 2 + q
                    rows_b[at : at + 1, :] = jnp.sum(
                        jnp.where(gap2[rows, :] == float(b), cross[rows, :], 0.0),
                        axis=0,
                        keepdims=True,
                    )
        high = lax.Precision.HIGHEST
        grads = jnp.dot(rows_b[...], sel_b[...], precision=high, preferred_element_type=F32)
        at_row = lax.broadcasted_iota(jnp.int32, (24, 128), 0)
        at_lane = lax.broadcasted_iota(jnp.int32, (24, 128), 1)
        own_f = own.astype(F32)
        for q in range(2):
            spot = jnp.logical_and(at_row == 18, at_lane == 32 + q)
            grads += jnp.where(spot, jnp.sum(own_f[q * BLK : (q + 1) * BLK]), 0.0)
        gsec[...] = grads

    arrived(krecv, k_r)
    low_rows = lax.broadcasted_iota(jnp.int32, (8, MR), 0) < 4
    low_lanes = lax.broadcasted_iota(jnp.int32, (8, 128), 1) < 64

    def pick(values, index):
        return jnp.take_along_axis(values, index, axis=1, mode="promise_in_bounds")

    def expand(s, _):
        got = krecv[s].astype(F32)
        halves = []
        for zhi in range(2):
            first = pos[pl.ds(s * 4 + 2 * zhi, 1), :]
            second = pos[pl.ds(s * 4 + 2 * zhi + 1, 1), :]
            index = jnp.where(
                low_rows,
                jnp.broadcast_to(first, (8, MR)),
                jnp.broadcast_to(second, (8, MR)),
            )
            at = [index[:, j * 128 : (j + 1) * 128] for j in range(5)]
            re, im = got[0:8], got[8:16]
            halves.append(
                jnp.concatenate(
                    [
                        pick(re, at[0]),
                        pick(re, at[1]),
                        jnp.where(low_lanes, pick(re, at[2]), pick(im, at[2])),
                        pick(im, at[3]),
                        pick(im, at[4]),
                    ],
                    axis=1,
                )
            )
        ex[pl.ds(pl.multiple_of(s * 16, 16), 16), :] = jnp.concatenate(halves, axis=0).astype(BF)
        return 0

    lax.fori_loop(0, NS, expand, 0, unroll=2)

    def k_y(g, _):
        rows = pl.ds(pl.multiple_of(g * 256, 256), 256)
        half = mm(ex[rows, :], ty[...]).astype(BF).astype(F32)
        for j in range(5):
            hsc[j, rows, :] = half[:, j * 128 : (j + 1) * 128]
        return 0

    lax.fori_loop(0, 4, k_y, 0)
    for j in range(NCH):
        to_image(0, j)
        coil_send(0, j)

    def take_cot(n):
        lo, hi = GROUPS[n]
        arrived(crecv[n], c_r.at[n])
        for j in range(lo, hi):
            lanes = slice((j - lo) * 128, (j - lo + 1) * 128)
            hsc[j] = crecv[n][:, :, lanes].astype(F32).reshape(16 * NS, 128)
            to_image(1, j)
            coil_send(1, j)

    take_cot(0)
    coil_sum(0, 0)
    coil_sum(0, 1)
    take_cot(1)
    windows(0)
    into_hidden(0, w1b)

    def activate(g, _):
        rows = pl.ds(pl.multiple_of(g * 16, 16), 16)
        kind = edge[rows, :]
        add = bcol[rows, :]
        for x3 in range(3):
            for blk in range(NB):
                lanes = slice((x3 * NB + blk) * 128, (x3 * NB + blk + 1) * 128)
                h = hid[0, rows, lanes] + add
                s = 0.5 * jnp.tanh(0.5 * h) + 0.5
                act[rows, lanes] = keep(h * s, kind, x3, blk).astype(BF)
                hid[0, rows, lanes] = s * (1.0 + h * (1.0 - s))
        return 0

    lax.fori_loop(0, MR // 16, activate, 0)
    regularized = out_of_hidden(act, w2b)
    for q in range(2):
        for blk in range(NB):
            block = regularized[q * BLK : (q + 1) * BLK, blk * 128 : (blk + 1) * 128] + b2_ref[q]
            agsend[0, q, blk * BLK : (blk + 1) * BLK, :] = block.astype(BF)
    gather_send(0)

    coil_sum(1, 0)
    take_cot(2)
    coil_sum(1, 1)
    second_grad()

    arrived(agrecv.at[0], ag_r.at[0])

    def quarters(g):
        for half_y in range(2):
            for half_z in range(2):
                src = pl.ds(pl.multiple_of(g * 16, 16), 16)
                dst = pl.ds(pl.multiple_of(half_y * 160 + g * 16, 16), 16)
                lo = slice(half_z * 128, half_z * 128 + 128)
                hi = slice(NZ + half_z * 128, NZ + half_z * 128 + 128)
                yield half_z * 2 + half_y, src, dst, lo, hi

    def begin(g, _):
        for slot, src, dst, lo, hi in quarters(g):
            r0 = agrecv[0, slot, 0, src, :].astype(F32)
            r1 = agrecv[0, slot, 1, src, :].astype(F32)
            for c in range(CL):
                k0 = img[1, c, dst, lo].astype(F32)
                k1 = img[1, c, dst, hi].astype(F32)
                regpart[0, c, dst, lo] = k0 * r0 + k1 * r1
                regpart[1, c, dst, lo] = k1 * r0 - k0 * r1
        return 0

    lax.fori_loop(0, 10, begin, 0)
    windows(1)
    into_hidden(1, w2f)

    def grad_hidden(g, _):
        rows = pl.ds(pl.multiple_of(g * 16, 16), 16)
        kind = edge[rows, :]
        for x3 in range(3):
            for blk in range(NB):
                lanes = slice((x3 * NB + blk) * 128, (x3 * NB + blk + 1) * 128)
                value = hid[1, rows, lanes] * hid[0, rows, lanes]
                gp[rows, lanes] = keep(value, kind, x3, blk).astype(BF)
        return 0

    lax.fori_loop(0, MR // 16, grad_hidden, 0)
    grad_comb = out_of_hidden(gp, w1f)
    for q in range(2):
        for blk in range(NB):
            block = grad_comb[q * BLK : (q + 1) * BLK, blk * 128 : (blk + 1) * 128]
            agsend[1, q, blk * BLK : (blk + 1) * BLK, :] = block.astype(BF)
    gather_send(1)

    rows_a[...] = jnp.zeros((24, MR), F32)
    gp_mid = gp[:, LN : 2 * LN]
    cross = mm_nt(vbuf[0, :, LN : 2 * LN], gp_mid)
    for i in range(2):
        for a in range(3):
            rows = slice((i * 3 + a) * US, (i * 3 + a + 1) * US)
            block = cross[rows, :]
            gap = gap3[rows, :]
            for b in range(3):
                at = (a * 3 + b) * 2 + i
                rows_a[at : at + 1, :] = jnp.sum(
                    jnp.where(gap == float(b), block, 0.0), axis=0, keepdims=True
                )
    sums = mm_nt(jnp.ones((8, LN), BF), gp_mid) * middle[...]
    rows_a[18:19, :] = sums[0:1, :]
    high = lax.Precision.HIGHEST
    grads = jnp.dot(rows_a[...], sel_a[...], precision=high, preferred_element_type=F32)
    grads += gsec[...]
    def share(n, buf, count, mine, device):
        buf[mine] = grads_in[n]
        for j in range(1, count):
            to = lax.rem(mine + j, count)
            pltpu.make_async_remote_copy(
                src_ref=buf.at[mine],
                dst_ref=buf.at[mine],
                send_sem=ar_s.at[n],
                recv_sem=ar_r.at[n],
                device_id=device(to),
                device_id_type=MESH,
            ).start()

    def collect(n, buf, count):
        arrived(buf.at[pl.ds(0, count - 1)], ar_r.at[n])
        total = buf[0]
        for j in range(1, count):
            total += buf[j]
        return total

    grads_in = [grads]
    share(0, ar1, 16, row_zc, lambda to: (row_y * 16 + to, co))

    arrived(agrecv.at[1], ag_r.at[1])

    def result(half):
        def finish(g, _):
            for slot, src, dst, lo, hi in quarters(g):
                g0 = agrecv[1, slot, 0, src, :].astype(F32)
                g1 = agrecv[1, slot, 1, src, :].astype(F32)
                for c in range(half * 2, half * 2 + 2):
                    i0 = img[0, c, dst, lo].astype(F32)
                    i1 = img[0, c, dst, hi].astype(F32)
                    re = i0 * g0 + i1 * g1 - regpart[0, c, dst, lo]
                    im = i1 * g0 - i0 * g1 - regpart[1, c, dst, lo]
                    outv[0, c, dst, lo] = re.astype(BF)
                    outv[1, c, dst, lo] = im.astype(BF)
            return 0

        lax.fori_loop(0, 10, finish, 0)
        for p in range(2):
            store(p, half).start()

    def store(p, half):
        coils = pl.ds(half * 2, 2)
        return pltpu.make_async_copy(
            outv.at[p, coils], pre_hbm.at[p, coils], o_sem.at[p * 2 + half]
        )

    result(0)

    grads_in.append(collect(0, ar1, 16))
    share(1, ar2, 16, row_y * 4 + co, lambda to: (to // 4 * 16 + row_zc, to % 4))
    result(1)
    gw_ref[...] = collect(1, ar2, 16) * (1.0 / math.sqrt(NS * NY * NZ))

    arrived(ksend.at[pl.ds(0, NS - 1)], k_s)
    for n in range(len(GROUPS)):
        arrived(csend[n].at[pl.ds(0, NS - 1)], c_s.at[n])
    for n in range(2):
        for step, (first, count) in enumerate(STEPS):
            arrived(rsrecv.at[n, pl.ds(0, 3), :, pl.ds(first, count)], rs_s.at[n, step])
            arrived(hrecv.at[n, pl.ds(0, 4), :, pl.ds(first, count)], h_s.at[n, step])
        arrived(agrecv.at[n, pl.ds(0, NCOIL - 1)], ag_s.at[n])
    arrived(ar1.at[pl.ds(0, 15)], ar_s.at[0])
    arrived(ar2.at[pl.ds(0, 15)], ar_s.at[1])
    for p in range(2):
        for half in range(2):
            store(p, half).wait()


def final_kernel(pre_hbm, gw_ref, out_hbm, g1_ref, gb1_ref, g2_ref, gb2_ref, held, sem_in, sem_out):
    spots = [(p, c) for p in range(2) for c in range(CL)]
    loads = [pltpu.make_async_copy(pre_hbm.at[s], held.at[s], sem_in.at[s]) for s in spots]
    stores = [pltpu.make_async_copy(held.at[s], out_hbm.at[s], sem_out.at[s]) for s in spots]
    for load in loads:
        load.start()
    second = pltpu.roll(gw_ref[...], 96, 1)
    for a in range(3):
        for b in range(3):
            at = (a * 3 + b) * 2
            g1_ref[a, b] = gw_ref[at : at + 2, 0:CH]
            g2_ref[a, b] = second[at : at + 2, 0:CH]
    gb1_ref[...] = gw_ref[18:19, 0:CH]
    gb2_ref[...] = second[18:19, 0:2]
    for load, store in zip(loads, stores):
        load.wait()
        store.start()
    for store in stores:
        store.wait()


def on_device(k_space, cotangent, sens_maps, line_index, w_first, b_first, w_second, b_second):
    constants = make_constants()
    sens = jnp.transpose(sens_maps.reshape(2, CL, NZ, NY), (0, 1, 3, 2))
    index = jnp.transpose(line_index)
    first = jnp.transpose(w_first, (2, 3, 1, 0))
    second = jnp.transpose(w_second, (2, 3, 0, 1))
    vm = pl.BlockSpec(memory_space=pltpu.VMEM)
    anym = pl.BlockSpec(memory_space=pl.ANY)
    dma = pltpu.SemaphoreType.DMA
    scratch = [pltpu.VMEM(c.shape, c.dtype) for c in constants]
    scratch += [
        pltpu.VMEM((2, CL, ZL, NS, NY), BF),
        pltpu.VMEM((2, CL, ZL, NS, NY), BF),
        pltpu.VMEM((2, CL, NY, NZ), BF),
        pltpu.VMEM((16 * NS, 128), F32),
        pltpu.VMEM((NS, 16, 128), BF),
        pltpu.VMEM((NS, 16, 128), BF),
        pltpu.VMEM((5, 16 * NS, 128), F32),
        *[pltpu.VMEM((NS, 16, 128 * (hi - lo)), BF) for lo, hi in GROUPS],
        *[pltpu.VMEM((NS, 16, 128 * (hi - lo)), BF) for lo, hi in GROUPS],
        pltpu.VMEM((NZ, 640), jnp.int32),
        pltpu.VMEM((NZ * CL, 640), BF),
        pltpu.VMEM((5, NZ * CL, 128), F32),
        pltpu.VMEM((2, CL, NY, 2 * NZ), BF),
        pltpu.VMEM((2, 2, NY, NZ), BF),
        pltpu.VMEM((2, NCOIL, 2, PR, 128), BF),
        pltpu.VMEM((2, 5, 2, PR, 128), BF),
        pltpu.VMEM((5, 2, TR, 128), F32),
        pltpu.VMEM((2, KR, 3 * LN), BF),
        pltpu.VMEM((2, MR, 3 * LN), F32),
        pltpu.VMEM((MR, 3 * LN), BF),
        pltpu.VMEM((MR, 3 * LN), BF),
        pltpu.VMEM((MR, 128), F32),
        pltpu.VMEM((MR, KR), BF),
        pltpu.VMEM((MR, KR), BF),
        pltpu.VMEM((3, 64, MR), BF),
        pltpu.VMEM((3, 64, MR), BF),
        pltpu.VMEM((2, 2, NY // 2, 128), BF),
        pltpu.VMEM((2, NCOIL, 2, NY // 2, 128), BF),
        pltpu.VMEM((2, CL, NY, NZ), F32),
        pltpu.VMEM((2, CL, NY, NZ), BF),
        pltpu.VMEM((24, MR), F32),
        pltpu.VMEM((24, MR), F32),
        pltpu.VMEM((24, 128), F32),
        pltpu.VMEM((16, 24, 128), F32),
        pltpu.VMEM((16, 24, 128), F32),
        pltpu.VMEM((NZ, 128), jnp.int32),
        pltpu.VMEM((NZ, 128), jnp.int32),
        pltpu.VMEM((2, 128, 128), F32),
        dma((3,)),
        dma((len(constants),)),
        dma((4,)),
        dma,
        dma,
        dma((len(GROUPS),)),
        dma((len(GROUPS),)),
        dma((2, 2)),
        dma((2, 2)),
        dma((2, 2)),
        dma((2, 2)),
        dma((2,)),
        dma((2,)),
        dma((2,)),
        dma((2,)),
    ]
    smem = pl.BlockSpec(memory_space=pltpu.SMEM)
    result, grads = pl.pallas_call(
        cascade_kernel,
        out_shape=(
            jax.ShapeDtypeStruct((2, CL, NY, NZ), BF),
            jax.ShapeDtypeStruct((24, 128), F32),
        ),
        in_specs=[anym] * 3 + [vm] * 3 + [smem] * 2 + [anym] * len(constants),
        out_specs=(anym, vm),
        scratch_shapes=scratch,
        compiler_params=pltpu.CompilerParams(
            collective_id=0, has_side_effects=True, vmem_limit_bytes=60 * 1024 * 1024
        ),
    )(k_space, cotangent, sens, index, first, second, b_first, b_second, *constants)
    grad_sens, grad_w1, grad_b1, grad_w2, grad_b2 = pl.pallas_call(
        final_kernel,
        out_shape=(
            jax.ShapeDtypeStruct((2, CL, NY, NZ), BF),
            jax.ShapeDtypeStruct((3, 3, 2, CH), F32),
            jax.ShapeDtypeStruct((1, CH), F32),
            jax.ShapeDtypeStruct((3, 3, 2, CH), F32),
            jax.ShapeDtypeStruct((1, 2), F32),
        ),
        in_specs=[anym, vm],
        out_specs=(anym, vm, vm, vm, vm),
        scratch_shapes=[pltpu.VMEM((2, CL, NY, NZ), BF), dma((2, CL)), dma((2, CL))],
        compiler_params=pltpu.CompilerParams(vmem_limit_bytes=60 * 1024 * 1024),
    )(result, grads)
    grad_sens = jnp.transpose(grad_sens, (0, 1, 3, 2)).reshape(2, CL, NZ, 1, NY)
    grad_w1 = jnp.transpose(grad_w1, (3, 2, 0, 1))
    grad_w2 = jnp.transpose(grad_w2, (2, 3, 0, 1))
    grad_b1 = grad_b1.reshape(CH)
    grad_b2 = grad_b2.reshape(2)
    return (grad_sens, grad_w1, grad_b1, grad_w2, grad_b2)


def solution(mesh):
    placed = (
        P(None, "coil", "space", None, None),
        P(None, "coil", "space", None, None),
        P(None, "coil", None, "space", None),
        P(),
        P(),
        P(),
        P(),
        P(),
    )
    return jax.shard_map(
        on_device,
        mesh=mesh,
        in_specs=placed,
        out_specs=(P(None, "coil", None, "space", None), P(), P(), P(), P()),
        check_vma=False,
    )
```

```python
import math

import jax
import jax.numpy as jnp
import numpy as np
import ml_dtypes
from jax import lax
from jax.experimental import pallas as pl
from jax.experimental.pallas import tpu as pltpu
from jax.sharding import PartitionSpec as P

MESH = pl.DeviceIdType.MESH
BF = jnp.bfloat16
F32 = jnp.float32
NS, NCOIL = 64, 4
NY, NZ, CH, LINES = 320, 256, 18, 40
CL, ZL = 4, 4
BLK, NB = 32, 5
HV, HU, US = 34, 36, 40
MR, KR = 640, 256
PR = 176
TR = 192
LN = NB * 128
NCH = 5
GROUPS = ((0, 2), (2, 4), (4, 5))
PIECES = (
    (0, 0, 0, 64, 0),
    (1, 0, 64, 48, 0),
    (1, 0, 112, 16, 1),
    (2, 0, 128, 48, 1),
    (2, 1, 144, 48, 0),
    (3, 1, 192, 64, 0),
    (4, 1, 256, 64, 1),
)
BLOCKS = ((0, 2), (2, 5))
STEPS = ((0, 112), (112, 64))


def one_hot(rows, cols, pairs):
    table = np.zeros((rows, cols), np.float32)
    for r, c in pairs:
        table[r, c] = 1.0
    return table


def dft_matrix(length):
    position = np.arange(length)
    angles = 2.0 * math.pi / length * ((position[:, None] * position[None, :]) % length)
    cosine = np.cos(angles) / math.sqrt(length)
    sine = np.sin(angles) / math.sqrt(length)
    return np.block([[cosine, sine], [-sine, cosine]]).astype(ml_dtypes.bfloat16)


def make_constants():
    bf = ml_dtypes.bfloat16
    table_y = dft_matrix(NY).reshape(2 * NY, 2, NCH, 64)
    table_y = np.ascontiguousarray(table_y.transpose(0, 2, 1, 3)).reshape(2 * NY, 2 * NY)
    hid = [(ch * HV + v, ch, v) for ch in range(CH) for v in range(HV)]
    inp = [((i * 3 + a) * US + u, i, a, u) for i in range(2) for a in range(3) for u in range(HU)]
    spread = one_hot(MR, 128, [(r, ch) for r, ch, _ in hid])
    pick1 = np.stack(
        [one_hot(128, KR, [((a * 3 + b) * 2 + i, r) for r, i, a, _ in inp]) for b in range(3)]
    )
    pick2 = np.stack(
        [
            one_hot(128, KR, [((8 - a * 3 - b) * 2 + i, r) for r, i, a, _ in inp])
            for b in range(3)
        ]
    )
    rowpick = np.stack(
        [
            one_hot(
                64, 128, [(q * BLK + t, (a * 3 + b) * 2 + q) for q in range(2) for t in range(BLK)]
            )
            for a in range(3)
            for b in range(3)
        ]
    )
    gap1 = np.full((MR, KR), 99.0, np.float32)
    for r, _, v in hid:
        for s, _, _, u in inp:
            gap1[r, s] = u - v
    gap2 = np.full((64, MR), 99.0, np.float32)
    for q in range(2):
        for t in range(BLK):
            for r, _, v in hid:
                gap2[q * BLK + t, r] = v - t
    inner = np.zeros((MR,), bool)
    for r, _, v in hid:
        inner[r] = 1 <= v <= BLK
    gap3 = np.where(inner[None, :], gap1.T, 99.0).astype(np.float32)
    sel_a = spread
    sel_b = np.roll(spread, CH, axis=1)
    middle = np.broadcast_to(inner[None, :], (8, MR)).astype(np.float32)
    edge = np.zeros((MR, 128), np.float32)
    for r, _, v in hid:
        edge[r] = 1.0 if v == 0 else 2.0 if v == HV - 1 else 0.0
    return [
        table_y,
        dft_matrix(NZ),
        spread.astype(bf),
        np.ascontiguousarray(spread.T).astype(bf),
        pick1.astype(bf),
        pick2.astype(bf),
        rowpick.astype(bf),
        gap1,
        gap2,
        gap3,
        sel_a,
        sel_b,
        middle,
        edge,
    ]


def mm(a, b):
    return jnp.dot(a, b, preferred_element_type=F32)


def mm_nt(a, b):
    return lax.dot_general(a, b, (((1,), (1,)), ((), ())), preferred_element_type=F32)


def arrived(ref, sem):
    pltpu.make_async_copy(ref, ref, sem).wait()


def cascade_kernel(*refs):
    n_const = 14
    k_hbm, cot_hbm, sens_hbm, index_ref, first_ref, second_ref, b1_ref, b2_ref = refs[:8]
    const_hbm = refs[8 : 8 + n_const]
    pre_hbm, gw_ref = refs[8 + n_const : 10 + n_const]
    rest = refs[10 + n_const :]
    consts = rest[:n_const]
    (
        kv, cv, sv, ksc, ksend, krecv, csc, cs0, cs1, cs2, cr0, cr1, cr2, pos, ex, hsc,
        img, part, rsrecv, hrecv, tmp, vbuf, hid, act, gp, bcol,
        w1b, w2f, w2b, w1f, agsend, agrecv, regpart, outv, rows_a, rows_b, gsec, ar1, ar2, lines_ref, lines2_ref, wt,
        ld_sem, c_ld, o_sem, k_s, k_r, c_s, c_r, rs_s, rs_r, h_s, h_r, ag_s, ag_r, ar_s, ar_r,
    ) = rest[n_const:]
    (ty, tz, spread, spread_t, pick1, pick2, rowpick, gap1, gap2, gap3, sel_a, sel_b, middle, edge) = consts

    csend, crecv = (cs0, cs1, cs2), (cr0, cr1, cr2)
    me = lax.axis_index("space")
    co = lax.axis_index("coil")
    hz = co // 2
    hy = co % 2

    barrier = pltpu.get_barrier_semaphore()

    def greet(j, _):
        pl.semaphore_signal(
            barrier, inc=1, device_id=(lax.rem(me + j, NS), co), device_id_type=MESH
        )
        return 0

    lax.fori_loop(1, NS, greet, 0)
    for j in range(1, NCOIL):
        pl.semaphore_signal(
            barrier, inc=1, device_id=(me, lax.rem(co + j, NCOIL)), device_id_type=MESH
        )
    row_y, row_zc = me // 16, me % 16
    for jy in range(1, 4):
        for jc in range(1, NCOIL):
            there = (lax.rem(row_y + jy, 4) * 16 + row_zc, lax.rem(co + jc, NCOIL))
            pl.semaphore_signal(barrier, inc=1, device_id=there, device_id_type=MESH)
    load_k = pltpu.make_async_copy(k_hbm, kv, ld_sem.at[0])
    load_c = pltpu.make_async_copy(cot_hbm, cv, ld_sem.at[1])
    load_s = pltpu.make_async_copy(sens_hbm, sv, ld_sem.at[2])
    load_k.start()
    load_c.start()
    loads = [
        pltpu.make_async_copy(src, dst, c_ld.at[n])
        for n, (src, dst) in enumerate(zip(const_hbm, consts))
    ]
    for load in loads:
        load.start()
    load_s.start()

    turned = jnp.concatenate(
        [index_ref[...].astype(F32), jnp.full((128 - LINES, NZ), -1.0, F32)], axis=0
    )
    shifted = jnp.concatenate(
        [jnp.full((64, NZ), -1.0, F32), turned[0:64]], axis=0
    )
    late = lax.broadcasted_iota(jnp.int32, (128, NZ), 1) % 4 >= 2
    lines_ref[...] = turned.T.astype(jnp.int32)
    lines2_ref[...] = jnp.where(late, shifted, turned).T.astype(jnp.int32)
    load_k.wait()
    y_rows = lax.broadcasted_iota(jnp.int32, (NY, 128), 0)

    def hot(z):
        row = lines2_ref[pl.ds(me * ZL + z, 1), :]
        return jnp.where(y_rows == row, 1.0, 0.0).astype(BF)

    hots = [hot(z) for z in range(ZL)]
    for p in range(2):
        for zlo in range(2):
            packed = mm(kv[p, :, zlo].reshape(CL * NS, NY), hots[zlo])
            packed += mm(kv[p, :, zlo + 2].reshape(CL * NS, NY), hots[zlo + 2])
            ksc[pl.ds((p * 2 + zlo) * 256, 256), :] = packed

    def pack_k(x, _):
        ksend[x] = ksc[pl.ds(x, 16, stride=NS), :].astype(BF)
        return 0

    lax.fori_loop(0, NS, pack_k, 0, unroll=4)

    def spread_out(src, dst, s_sem, r_sem):
        pltpu.make_async_copy(src.at[me], dst.at[me], r_sem).start()

        def send(j, _):
            to = lax.rem(me + j, NS)
            pltpu.make_async_remote_copy(
                src_ref=src.at[to],
                dst_ref=dst.at[me],
                send_sem=s_sem,
                recv_sem=r_sem,
                device_id=(to, co),
                device_id_type=MESH,
            ).start()
            return 0

        lax.fori_loop(1, NS, send, 0)

    pl.semaphore_wait(barrier, NS - 1 + NCOIL - 1 + 9)
    spread_out(ksend, krecv, k_s, k_r)

    load_c.wait()
    loads[0].wait()

    def cot_y(zl, _):
        rows = mm(cv[0, :, zl].reshape(CL * NS, NY), ty[0:NY])
        rows += mm(cv[1, :, zl].reshape(CL * NS, NY), ty[NY:])
        for j in range(5):
            csc[j, pl.ds(pl.multiple_of(zl * 256, 256), 256), :] = rows[:, j * 128 : (j + 1) * 128]
        return 0

    lax.fori_loop(0, ZL, cot_y, 0)

    def pack_c(x, _):
        for n, (lo, hi) in enumerate(GROUPS):
            for j in range(lo, hi):
                lanes = slice((j - lo) * 128, (j - lo + 1) * 128)
                csend[n][x, :, lanes] = csc[j, pl.ds(x, 16, stride=NS), :].astype(BF)
        return 0

    lax.fori_loop(0, NS, pack_c, 0, unroll=2)

    for n in range(len(GROUPS)):
        spread_out(csend[n], crecv[n], c_s.at[n], c_r.at[n])

    for load in loads[1:]:
        load.wait()
    lane_y = lax.broadcasted_iota(jnp.int32, (32, MR), 1)
    lane_y = jnp.where(lane_y >= NY, lane_y - NY, lane_y)
    upper = jnp.where(lax.broadcasted_iota(jnp.int32, (32, MR), 0) % 4 >= 2, 64, 0)

    def find(g, _):
        rows = pl.ds(pl.multiple_of(g * 32, 32), 32)
        lines = lines_ref[rows, :]
        place = jnp.full((32, MR), 127, jnp.int32)
        for line in range(LINES):
            place = jnp.where(lines[:, line : line + 1] == lane_y, upper + line, place)
        pos[rows, :] = place
        return 0

    lax.fori_loop(0, NZ // 32, find, 0)

    load_s.wait()

    def to_image(n, j):
        columns = []
        for c in range(CL):
            block = hsc[j, pl.ds(c, NZ, stride=CL), :].T.astype(BF)
            columns.append(jnp.concatenate([block[0:64], block[64:128]], axis=1))
        image = mm(jnp.concatenate(columns, axis=0), tz[...]).astype(BF)
        for c in range(CL):
            img[n, c, j * 64 : (j + 1) * 64, :] = image[c * 64 : (c + 1) * 64]

        def combine(g, _):
            rows = pl.ds(pl.multiple_of(j * 64 + g * 16, 16), 16)
            re = jnp.zeros((16, NZ), F32)
            im = jnp.zeros((16, NZ), F32)
            for c in range(CL):
                both = img[n, c, rows, :].astype(F32)
                i0, i1 = both[:, :NZ], both[:, NZ:]
                s0 = sv[0, c, rows, :].astype(F32)
                s1 = sv[1, c, rows, :].astype(F32)
                re += s0 * i0 + s1 * i1
                im += s0 * i1 - s1 * i0
            if n == 1:
                re, im = -re, -im
            part[n, 0, rows, :] = re.astype(BF)
            part[n, 1, rows, :] = im.astype(BF)
            return 0

        lax.fori_loop(0, 4, combine, 0)

    def coil_send(n, chunk):
        for j, half, row, count, step in PIECES:
            if j != chunk:
                continue
            for half_z in range(2):
                to = half_z * 2 + half
                src = part.at[n, :, pl.ds(row, count), pl.ds(half_z * 128, 128)]
                dst = rsrecv.at[n, co, :, pl.ds(row - half * 144, count)]

                @pl.when(co == to)
                def _():
                    pltpu.make_async_copy(src, dst, rs_r.at[n, step]).start()

                @pl.when(co != to)
                def _():
                    pltpu.make_async_remote_copy(
                        src_ref=src,
                        dst_ref=dst,
                        send_sem=rs_s.at[n, step],
                        recv_sem=rs_r.at[n, step],
                        device_id=(me, to),
                        device_id_type=MESH,
                    ).start()

    def coil_sum(n, step):
        first, count = STEPS[step]
        rows = slice(first, first + count)
        arrived(rsrecv.at[n, :, :, pl.ds(first, count)], rs_r.at[n, step])
        for q in range(2):
            total = rsrecv[n, 0, q, rows].astype(F32)
            for j in range(1, NCOIL):
                total += rsrecv[n, j, q, rows].astype(F32)
            hrecv[n, 4, q, rows] = total.astype(BF)
        for slot, off in enumerate((-2, -1, 1, 2)):
            to = lax.rem(me + off + NS, NS)
            pltpu.make_async_remote_copy(
                src_ref=hrecv.at[n, 4, :, pl.ds(first, count)],
                dst_ref=hrecv.at[n, 3 - slot, :, pl.ds(first, count)],
                send_sem=h_s.at[n, step],
                recv_sem=h_r.at[n, step],
                device_id=(to, co),
                device_id_type=MESH,
            ).start()

    def windows(n, step):
        first, count = STEPS[step]
        arrived(hrecv.at[n, pl.ds(0, 4), :, pl.ds(first, count)], h_r.at[n, step])
        for j, slot in enumerate((0, 1, 4, 2, 3)):
            x = me + j - 2
            inside = jnp.logical_and(x >= 0, x < NS)
            for q in range(2):
                got = hrecv[n, slot, q, first : first + count].astype(F32)
                tmp[j, q, 2 + first : 2 + first + count, :] = jnp.where(inside, got, 0.0)
        for x3 in range(3):
            for blk in range(*BLOCKS[step]):
                lanes = slice((x3 * NB + blk) * 128, (x3 * NB + blk + 1) * 128)
                rows = pl.ds(pl.multiple_of(hy * 16, 16) + blk * BLK, US)
                column = [tmp[x3 + a, q, rows, :] for q in range(2) for a in range(3)]
                vbuf[n, 0 : 6 * US, lanes] = jnp.concatenate(column, axis=0).astype(BF)

    def lanes_of(x3, step):
        lo, hi = BLOCKS[step]
        return slice(x3 * LN + lo * 128, x3 * LN + hi * 128)

    def into_hidden(n, w, step):
        for x3 in range(3):
            lanes = lanes_of(x3, step)
            hid[n, :, lanes] = mm(w[...], vbuf[n, :, lanes])

    x_ok = [jnp.logical_and(me + d >= 0, me + d < NS) for d in (-1, 0, 1)]

    def keep(value, kind, x3, blk):
        if blk == 0:
            value = jnp.where(jnp.logical_and(kind == 1.0, hy == 0), 0.0, value)
        if blk == NB - 1:
            value = jnp.where(jnp.logical_and(kind == 2.0, hy == 1), 0.0, value)
        if x3 != 1:
            value = jnp.where(x_ok[x3], value, 0.0)
        return value

    def out_of_hidden(values, w, step):
        total = mm(w[0], values[:, lanes_of(0, step)])
        total += mm(w[1], values[:, lanes_of(1, step)])
        total += mm(w[2], values[:, lanes_of(2, step)])
        return total

    def gather_send(n, step):
        lo, hi = BLOCKS[step]
        rows = pl.ds(lo * BLK, (hi - lo) * BLK)
        src = agsend.at[n, :, rows]
        dst = agrecv.at[n, co, :, rows]
        pltpu.make_async_copy(src, dst, ag_r.at[n, step]).start()
        for j in range(1, NCOIL):
            to = lax.rem(co + j, NCOIL)
            pltpu.make_async_remote_copy(
                src_ref=src,
                dst_ref=dst,
                send_sem=ag_s.at[n, step],
                recv_sem=ag_r.at[n, step],
                device_id=(me, to),
                device_id_type=MESH,
            ).start()

    def gathered(n):
        for step, (lo, hi) in enumerate(BLOCKS):
            arrived(agrecv.at[n, :, :, pl.ds(lo * BLK, (hi - lo) * BLK)], ag_r.at[n, step])

    def second_grad():
        rows_b[...] = jnp.zeros((24, MR), F32)
        own = jnp.concatenate(
            [
                jnp.concatenate(
                    [
                        hrecv[1, 4, q, pl.ds(pl.multiple_of(hy * 16, 16) + blk * BLK, BLK), :]
                        for blk in range(NB)
                    ],
                    axis=1,
                )
                for q in range(2)
            ],
            axis=0,
        )
        for a in range(3):
            cross = mm_nt(own, act[:, a * LN : (a + 1) * LN])
            for q in range(2):
                rows = slice(q * BLK, (q + 1) * BLK)
                for b in range(3):
                    at = a * 6 + b * 2 + q
                    rows_b[at : at + 1, :] = jnp.sum(
                        jnp.where(gap2[rows, :] == float(b), cross[rows, :], 0.0),
                        axis=0,
                        keepdims=True,
                    )
        high = lax.Precision.HIGHEST
        grads = jnp.dot(rows_b[...], sel_b[...], precision=high, preferred_element_type=F32)
        at_row = lax.broadcasted_iota(jnp.int32, (24, 128), 0)
        at_lane = lax.broadcasted_iota(jnp.int32, (24, 128), 1)
        own_f = own.astype(F32)
        for q in range(2):
            spot = jnp.logical_and(at_row == 18, at_lane == CH + q)
            grads += jnp.where(spot, jnp.sum(own_f[q * BLK : (q + 1) * BLK]), 0.0)
        gsec[...] = grads

    arrived(krecv, k_r)
    low_rows = lax.broadcasted_iota(jnp.int32, (8, MR), 0) < 4
    low_lanes = lax.broadcasted_iota(jnp.int32, (8, 128), 1) < 64

    def pick(values, index):
        return jnp.take_along_axis(values, index, axis=1, mode="promise_in_bounds")

    def expand(s, _):
        got = krecv[s].astype(F32)
        halves = []
        for zhi in range(2):
            first = pos[pl.ds(s * 4 + 2 * zhi, 1), :]
            second = pos[pl.ds(s * 4 + 2 * zhi + 1, 1), :]
            index = jnp.where(
                low_rows,
                jnp.broadcast_to(first, (8, MR)),
                jnp.broadcast_to(second, (8, MR)),
            )
            at = [index[:, j * 128 : (j + 1) * 128] for j in range(5)]
            re, im = got[0:8], got[8:16]
            halves.append(
                jnp.concatenate(
                    [
                        pick(re, at[0]),
                        pick(re, at[1]),
                        jnp.where(low_lanes, pick(re, at[2]), pick(im, at[2])),
                        pick(im, at[3]),
                        pick(im, at[4]),
                    ],
                    axis=1,
                )
            )
        ex[pl.ds(pl.multiple_of(s * 16, 16), 16), :] = jnp.concatenate(halves, axis=0).astype(BF)
        return 0

    lax.fori_loop(0, NS, expand, 0, unroll=8)

    def k_y(g, _):
        rows = pl.ds(pl.multiple_of(g * 256, 256), 256)
        half = mm(ex[rows, :], ty[...]).astype(BF).astype(F32)
        for j in range(5):
            hsc[j, rows, :] = half[:, j * 128 : (j + 1) * 128]
        return 0

    lax.fori_loop(0, 4, k_y, 0)
    for j in range(NCH):
        to_image(0, j)
        coil_send(0, j)

    def take_cot(n):
        lo, hi = GROUPS[n]
        arrived(crecv[n], c_r.at[n])
        for j in range(lo, hi):
            lanes = slice((j - lo) * 128, (j - lo + 1) * 128)
            hsc[j] = crecv[n][:, :, lanes].astype(F32).reshape(16 * NS, 128)
            to_image(1, j)
            coil_send(1, j)

    wt[...] = jnp.zeros((2, 128, 128), F32)
    for n, ref in enumerate((first_ref, second_ref)):
        for a in range(3):
            for b in range(3):
                at = (a * 3 + b) * 2
                wt[n, at : at + 2, 0:CH] = ref[a, b].astype(F32)
    w1 = wt[0].astype(BF)
    w2 = wt[1].astype(BF)
    sp = spread[...]
    spt = spread_t[...]
    by_hidden1 = mm_nt(sp, w1).astype(BF)
    by_hidden2 = mm_nt(sp, w2).astype(BF)
    band1 = jnp.zeros((MR, KR), F32)
    band2 = jnp.zeros((MR, KR), F32)
    for b in range(3):
        hit = gap1[...] == float(b)
        band1 += jnp.where(hit, mm(by_hidden1, pick1[b]), 0.0)
        band2 += jnp.where(hit, mm(by_hidden2, pick2[b]), 0.0)
    w1b[...] = band1.astype(BF)
    w2f[...] = band2.astype(BF)
    for a in range(3):
        out2 = jnp.zeros((64, MR), F32)
        out1 = jnp.zeros((64, MR), F32)
        for b in range(3):
            hit = gap2[...] == float(b)
            out2 += jnp.where(hit, mm(mm(rowpick[a * 3 + b], w2).astype(BF), spt), 0.0)
            flipped = rowpick[(2 - a) * 3 + (2 - b)]
            out1 += jnp.where(hit, mm(mm(flipped, w1).astype(BF), spt), 0.0)
        w2b[a] = out2.astype(BF)
        w1f[a] = out1.astype(BF)
    lane = lax.broadcasted_iota(jnp.int32, (1, 128), 1)
    row = jnp.zeros((1, 128), F32)
    for ch in range(CH):
        row = jnp.where(lane == ch, b1_ref[ch], row)
    bias = jnp.sum(sp.astype(F32) * row, axis=1, keepdims=True)
    bcol[...] = jnp.broadcast_to(bias, (MR, 128))
    zero_rows = jnp.zeros((KR - 6 * US, 3 * LN), BF)
    for n in range(2):
        vbuf[n, 6 * US :, :] = zero_rows
    for j in range(5):
        for i in range(2):
            tmp[j, i, 0:8, :] = jnp.zeros((8, 128), F32)
            tmp[j, i, 176:TR, :] = jnp.zeros((TR - 176, 128), F32)

    coil_sum(0, 0)
    coil_sum(0, 1)
    take_cot(0)
    take_cot(1)
    take_cot(2)
    coil_sum(1, 0)
    for step in range(2):
        windows(0, step)
        into_hidden(0, w1b, step)

    def activate(g, _):
        rows = pl.ds(pl.multiple_of(g * 16, 16), 16)
        kind = edge[rows, :]
        add = bcol[rows, :]
        for x3 in range(3):
            for blk in range(NB):
                lanes = slice((x3 * NB + blk) * 128, (x3 * NB + blk + 1) * 128)
                h = hid[0, rows, lanes] + add
                s = 0.5 * jnp.tanh(0.5 * h) + 0.5
                act[rows, lanes] = keep(h * s, kind, x3, blk).astype(BF)
                hid[0, rows, lanes] = s * (1.0 + h * (1.0 - s))
        return 0

    lax.fori_loop(0, MR // 16, activate, 0)
    for step, (lo, hi) in enumerate(BLOCKS):
        regularized = out_of_hidden(act, w2b, step)
        for q in range(2):
            for blk in range(lo, hi):
                lanes = slice((blk - lo) * 128, (blk - lo + 1) * 128)
                block = regularized[q * BLK : (q + 1) * BLK, lanes] + b2_ref[q]
                agsend[0, q, blk * BLK : (blk + 1) * BLK, :] = block.astype(BF)
        gather_send(0, step)

    coil_sum(1, 1)
    second_grad()

    def grad_blocks(step):
        lo, hi = BLOCKS[step]
        windows(1, step)
        into_hidden(1, w2f, step)

        def grad_hidden(g, _):
            rows = pl.ds(pl.multiple_of(g * 16, 16), 16)
            kind = edge[rows, :]
            for x3 in range(3):
                for blk in range(lo, hi):
                    lanes = slice((x3 * NB + blk) * 128, (x3 * NB + blk + 1) * 128)
                    value = hid[1, rows, lanes] * hid[0, rows, lanes]
                    gp[rows, lanes] = keep(value, kind, x3, blk).astype(BF)
            return 0

        lax.fori_loop(0, MR // 16, grad_hidden, 0, unroll=2)
        grad_comb = out_of_hidden(gp, w1f, step)
        for q in range(2):
            for blk in range(lo, hi):
                lanes = slice((blk - lo) * 128, (blk - lo + 1) * 128)
                block = grad_comb[q * BLK : (q + 1) * BLK, lanes]
                agsend[1, q, blk * BLK : (blk + 1) * BLK, :] = block.astype(BF)
        gather_send(1, step)

    grad_blocks(0)
    grad_blocks(1)

    gathered(0)

    def quarters(g):
        for half_y in range(2):
            for half_z in range(2):
                src = pl.ds(pl.multiple_of(g * 16, 16), 16)
                dst = pl.ds(pl.multiple_of(half_y * 160 + g * 16, 16), 16)
                lo = slice(half_z * 128, half_z * 128 + 128)
                hi = slice(NZ + half_z * 128, NZ + half_z * 128 + 128)
                yield half_z * 2 + half_y, src, dst, lo, hi

    def begin(g, _):
        for slot, src, dst, lo, hi in quarters(g):
            r0 = agrecv[0, slot, 0, src, :].astype(F32)
            r1 = agrecv[0, slot, 1, src, :].astype(F32)
            for c in range(CL):
                k0 = img[1, c, dst, lo].astype(F32)
                k1 = img[1, c, dst, hi].astype(F32)
                regpart[0, c, dst, lo] = k0 * r0 + k1 * r1
                regpart[1, c, dst, lo] = k1 * r0 - k0 * r1
        return 0

    rows_a[...] = jnp.zeros((24, MR), F32)
    gp_mid = gp[:, LN : 2 * LN]
    cross = mm_nt(vbuf[0, :, LN : 2 * LN], gp_mid)
    for i in range(2):
        for a in range(3):
            rows = slice((i * 3 + a) * US, (i * 3 + a + 1) * US)
            block = cross[rows, :]
            gap = gap3[rows, :]
            for b in range(3):
                at = (a * 3 + b) * 2 + i
                rows_a[at : at + 1, :] = jnp.sum(
                    jnp.where(gap == float(b), block, 0.0), axis=0, keepdims=True
                )
    sums = mm_nt(jnp.ones((8, LN), BF), gp_mid) * middle[...]
    rows_a[18:19, :] = sums[0:1, :]
    high = lax.Precision.HIGHEST
    grads = jnp.dot(rows_a[...], sel_a[...], precision=high, preferred_element_type=F32)
    grads += gsec[...]
    def share(n, buf, count, mine, device):
        buf[mine] = grads_in[n]
        for j in range(1, count):
            to = lax.rem(mine + j, count)
            pltpu.make_async_remote_copy(
                src_ref=buf.at[mine],
                dst_ref=buf.at[mine],
                send_sem=ar_s.at[n],
                recv_sem=ar_r.at[n],
                device_id=device(to),
                device_id_type=MESH,
            ).start()

    def collect(n, buf, count):
        arrived(buf.at[pl.ds(0, count - 1)], ar_r.at[n])
        total = buf[0]
        for j in range(1, count):
            total += buf[j]
        return total

    grads = grads[0:8] + pltpu.roll(grads[8:16], 36, 1) + pltpu.roll(grads[16:24], 72, 1)
    grads_in = [grads]
    share(0, ar1, 16, row_zc, lambda to: (row_y * 16 + to, co))

    lax.fori_loop(0, 10, begin, 0)
    grads_in.append(collect(0, ar1, 16))
    share(1, ar2, 16, row_y * 4 + co, lambda to: (to // 4 * 16 + row_zc, to % 4))
    gathered(1)

    def result(half):
        def finish(g, _):
            for slot, src, dst, lo, hi in quarters(g):
                g0 = agrecv[1, slot, 0, src, :].astype(F32)
                g1 = agrecv[1, slot, 1, src, :].astype(F32)
                for c in range(half * 2, half * 2 + 2):
                    i0 = img[0, c, dst, lo].astype(F32)
                    i1 = img[0, c, dst, hi].astype(F32)
                    re = i0 * g0 + i1 * g1 - regpart[0, c, dst, lo]
                    im = i1 * g0 - i0 * g1 - regpart[1, c, dst, lo]
                    outv[0, c, dst, lo] = re.astype(BF)
                    outv[1, c, dst, lo] = im.astype(BF)
            return 0

        lax.fori_loop(0, 10, finish, 0)
        for p in range(2):
            store(p, half).start()

    def store(p, half):
        coils = pl.ds(half * 2, 2)
        return pltpu.make_async_copy(
            outv.at[p, coils], pre_hbm.at[p, coils], o_sem.at[p * 2 + half]
        )

    result(0)

    result(1)
    gw_ref[...] = collect(1, ar2, 16) * (1.0 / math.sqrt(NS * NY * NZ))

    arrived(ksend.at[pl.ds(0, NS - 1)], k_s)
    for n in range(len(GROUPS)):
        arrived(csend[n].at[pl.ds(0, NS - 1)], c_s.at[n])
    for n in range(2):
        for step, (first, count) in enumerate(STEPS):
            arrived(rsrecv.at[n, pl.ds(0, 3), :, pl.ds(first, count)], rs_s.at[n, step])
            arrived(hrecv.at[n, pl.ds(0, 4), :, pl.ds(first, count)], h_s.at[n, step])
        for step, (lo, hi) in enumerate(BLOCKS):
            piece = agrecv.at[n, pl.ds(0, NCOIL - 1), :, pl.ds(lo * BLK, (hi - lo) * BLK)]
            arrived(piece, ag_s.at[n, step])
    arrived(ar1.at[pl.ds(0, 15)], ar_s.at[0])
    arrived(ar2.at[pl.ds(0, 15)], ar_s.at[1])
    for p in range(2):
        for half in range(2):
            store(p, half).wait()


def final_kernel(pre_hbm, gw_ref, out_hbm, g1_ref, gb1_ref, g2_ref, gb2_ref, held, sem_in, sem_out):
    spots = [(p, c) for p in range(2) for c in range(CL)]
    loads = [pltpu.make_async_copy(pre_hbm.at[s], held.at[s], sem_in.at[s]) for s in spots]
    stores = [pltpu.make_async_copy(held.at[s], out_hbm.at[s], sem_out.at[s]) for s in spots]
    for load in loads:
        load.start()
    folded = gw_ref[...]
    first = jnp.concatenate([folded, pltpu.roll(folded, 92, 1), pltpu.roll(folded, 56, 1)], axis=0)
    second = pltpu.roll(first, 128 - CH, 1)
    for a in range(3):
        for b in range(3):
            at = (a * 3 + b) * 2
            g1_ref[a, b] = first[at : at + 2, 0:CH]
            g2_ref[a, b] = second[at : at + 2, 0:CH]
    gb1_ref[...] = first[18:19, 0:CH]
    gb2_ref[...] = second[18:19, 0:2]
    for load, store in zip(loads, stores):
        load.wait()
        store.start()
    for store in stores:
        store.wait()


def on_device(k_space, cotangent, sens_maps, line_index, w_first, b_first, w_second, b_second):
    constants = make_constants()
    sens = jnp.transpose(sens_maps.reshape(2, CL, NZ, NY), (0, 1, 3, 2))
    index = jnp.transpose(line_index)
    first = jnp.transpose(w_first, (2, 3, 1, 0))
    second = jnp.transpose(w_second, (2, 3, 0, 1))
    vm = pl.BlockSpec(memory_space=pltpu.VMEM)
    anym = pl.BlockSpec(memory_space=pl.ANY)
    dma = pltpu.SemaphoreType.DMA
    scratch = [pltpu.VMEM(c.shape, c.dtype) for c in constants]
    scratch += [
        pltpu.VMEM((2, CL, ZL, NS, NY), BF),
        pltpu.VMEM((2, CL, ZL, NS, NY), BF),
        pltpu.VMEM((2, CL, NY, NZ), BF),
        pltpu.VMEM((16 * NS, 128), F32),
        pltpu.VMEM((NS, 16, 128), BF),
        pltpu.VMEM((NS, 16, 128), BF),
        pltpu.VMEM((5, 16 * NS, 128), F32),
        *[pltpu.VMEM((NS, 16, 128 * (hi - lo)), BF) for lo, hi in GROUPS],
        *[pltpu.VMEM((NS, 16, 128 * (hi - lo)), BF) for lo, hi in GROUPS],
        pltpu.VMEM((NZ, 640), jnp.int32),
        pltpu.VMEM((NZ * CL, 640), BF),
        pltpu.VMEM((5, NZ * CL, 128), F32),
        pltpu.VMEM((2, CL, NY, 2 * NZ), BF),
        pltpu.VMEM((2, 2, NY, NZ), BF),
        pltpu.VMEM((2, NCOIL, 2, PR, 128), BF),
        pltpu.VMEM((2, 5, 2, PR, 128), BF),
        pltpu.VMEM((5, 2, TR, 128), F32),
        pltpu.VMEM((2, KR, 3 * LN), BF),
        pltpu.VMEM((2, MR, 3 * LN), F32),
        pltpu.VMEM((MR, 3 * LN), BF),
        pltpu.VMEM((MR, 3 * LN), BF),
        pltpu.VMEM((MR, 128), F32),
        pltpu.VMEM((MR, KR), BF),
        pltpu.VMEM((MR, KR), BF),
        pltpu.VMEM((3, 64, MR), BF),
        pltpu.VMEM((3, 64, MR), BF),
        pltpu.VMEM((2, 2, NY // 2, 128), BF),
        pltpu.VMEM((2, NCOIL, 2, NY // 2, 128), BF),
        pltpu.VMEM((2, CL, NY, NZ), F32),
        pltpu.VMEM((2, CL, NY, NZ), BF),
        pltpu.VMEM((24, MR), F32),
        pltpu.VMEM((24, MR), F32),
        pltpu.VMEM((24, 128), F32),
        pltpu.VMEM((16, 8, 128), F32),
        pltpu.VMEM((16, 8, 128), F32),
        pltpu.VMEM((NZ, 128), jnp.int32),
        pltpu.VMEM((NZ, 128), jnp.int32),
        pltpu.VMEM((2, 128, 128), F32),
        dma((3,)),
        dma((len(constants),)),
        dma((4,)),
        dma,
        dma,
        dma((len(GROUPS),)),
        dma((len(GROUPS),)),
        dma((2, 2)),
        dma((2, 2)),
        dma((2, 2)),
        dma((2, 2)),
        dma((2, 2)),
        dma((2, 2)),
        dma((2,)),
        dma((2,)),
    ]
    smem = pl.BlockSpec(memory_space=pltpu.SMEM)
    result, grads = pl.pallas_call(
        cascade_kernel,
        out_shape=(
            jax.ShapeDtypeStruct((2, CL, NY, NZ), BF),
            jax.ShapeDtypeStruct((8, 128), F32),
        ),
        in_specs=[anym] * 3 + [vm] * 3 + [smem] * 2 + [anym] * len(constants),
        out_specs=(anym, vm),
        scratch_shapes=scratch,
        compiler_params=pltpu.CompilerParams(
            collective_id=0, has_side_effects=True, vmem_limit_bytes=60 * 1024 * 1024
        ),
    )(k_space, cotangent, sens, index, first, second, b_first, b_second, *constants)
    grad_sens, grad_w1, grad_b1, grad_w2, grad_b2 = pl.pallas_call(
        final_kernel,
        out_shape=(
            jax.ShapeDtypeStruct((2, CL, NY, NZ), BF),
            jax.ShapeDtypeStruct((3, 3, 2, CH), F32),
            jax.ShapeDtypeStruct((1, CH), F32),
            jax.ShapeDtypeStruct((3, 3, 2, CH), F32),
            jax.ShapeDtypeStruct((1, 2), F32),
        ),
        in_specs=[anym, vm],
        out_specs=(anym, vm, vm, vm, vm),
        scratch_shapes=[pltpu.VMEM((2, CL, NY, NZ), BF), dma((2, CL)), dma((2, CL))],
        compiler_params=pltpu.CompilerParams(vmem_limit_bytes=60 * 1024 * 1024),
    )(result, grads)
    grad_sens = jnp.transpose(grad_sens, (0, 1, 3, 2)).reshape(2, CL, NZ, 1, NY)
    grad_w1 = jnp.transpose(grad_w1, (3, 2, 0, 1))
    grad_w2 = jnp.transpose(grad_w2, (2, 3, 0, 1))
    grad_b1 = grad_b1.reshape(CH)
    grad_b2 = grad_b2.reshape(2)
    return (grad_sens, grad_w1, grad_b1, grad_w2, grad_b2)


def solution(mesh):
    placed = (
        P(None, "coil", "space", None, None),
        P(None, "coil", "space", None, None),
        P(None, "coil", None, "space", None),
        P(),
        P(),
        P(),
        P(),
        P(),
    )
    return jax.shard_map(
        on_device,
        mesh=mesh,
        in_specs=placed,
        out_specs=(P(None, "coil", None, "space", None), P(), P(), P(), P()),
        check_vma=False,
    )
```

```python
import math

import jax
import jax.numpy as jnp
import numpy as np
import ml_dtypes
from jax import lax
from jax.experimental import pallas as pl
from jax.experimental.pallas import tpu as pltpu
from jax.sharding import PartitionSpec as P

MESH = pl.DeviceIdType.MESH
BF = jnp.bfloat16
F32 = jnp.float32
NS, NCOIL = 64, 4
NY, NZ, CH, LINES = 320, 256, 18, 40
CL, ZL = 4, 4
BLK, NB = 32, 5
HV, HU, US = 34, 36, 40
MR, KR = 640, 256
PR = 176
TR = 192
LN = NB * 128
NCH = 5
GROUPS = ((0, 4), (4, 5))
PIECES = (
    (0, 0, 0, 64, 0),
    (1, 0, 64, 48, 0),
    (1, 0, 112, 16, 1),
    (2, 0, 128, 48, 1),
    (2, 1, 144, 48, 0),
    (3, 1, 192, 64, 0),
    (4, 1, 256, 64, 1),
)
BLOCKS = ((0, 2), (2, 5))
STEPS = ((0, 112), (112, 64))


def one_hot(rows, cols, pairs):
    table = np.zeros((rows, cols), np.float32)
    for r, c in pairs:
        table[r, c] = 1.0
    return table


def dft_matrix(length):
    position = np.arange(length)
    angles = 2.0 * math.pi / length * ((position[:, None] * position[None, :]) % length)
    cosine = np.cos(angles) / math.sqrt(length)
    sine = np.sin(angles) / math.sqrt(length)
    return np.block([[cosine, sine], [-sine, cosine]]).astype(ml_dtypes.bfloat16)


def make_constants():
    bf = ml_dtypes.bfloat16
    table_y = dft_matrix(NY).reshape(2 * NY, 2, NCH, 64)
    table_y = np.ascontiguousarray(table_y.transpose(0, 2, 1, 3)).reshape(2 * NY, 2 * NY)
    hid = [(ch * HV + v, ch, v) for ch in range(CH) for v in range(HV)]
    inp = [((i * 3 + a) * US + u, i, a, u) for i in range(2) for a in range(3) for u in range(HU)]
    spread = one_hot(MR, 128, [(r, ch) for r, ch, _ in hid])
    pick1 = np.stack(
        [one_hot(128, KR, [((a * 3 + b) * 2 + i, r) for r, i, a, _ in inp]) for b in range(3)]
    )
    pick2 = np.stack(
        [
            one_hot(128, KR, [((8 - a * 3 - b) * 2 + i, r) for r, i, a, _ in inp])
            for b in range(3)
        ]
    )
    rowpick = np.stack(
        [
            one_hot(
                64, 128, [(q * BLK + t, (a * 3 + b) * 2 + q) for q in range(2) for t in range(BLK)]
            )
            for a in range(3)
            for b in range(3)
        ]
    )
    gap1 = np.full((MR, KR), 99.0, np.float32)
    for r, _, v in hid:
        for s, _, _, u in inp:
            gap1[r, s] = u - v
    gap2 = np.full((64, MR), 99.0, np.float32)
    for q in range(2):
        for t in range(BLK):
            for r, _, v in hid:
                gap2[q * BLK + t, r] = v - t
    inner = np.zeros((MR,), bool)
    for r, _, v in hid:
        inner[r] = 1 <= v <= BLK
    gap3 = np.where(inner[None, :], gap1.T, 99.0).astype(np.float32)
    sel_a = spread
    sel_b = np.roll(spread, CH, axis=1)
    middle = np.broadcast_to(inner[None, :], (8, MR)).astype(np.float32)
    edge = np.zeros((MR, 128), np.float32)
    for r, _, v in hid:
        edge[r] = 1.0 if v == 0 else 2.0 if v == HV - 1 else 0.0
    return [
        table_y,
        dft_matrix(NZ),
        spread.astype(bf),
        np.ascontiguousarray(spread.T).astype(bf),
        pick1.astype(bf),
        pick2.astype(bf),
        rowpick.astype(bf),
        gap1,
        gap2,
        gap3,
        sel_a,
        sel_b,
        middle,
        edge,
    ]


def mm(a, b):
    return jnp.dot(a, b, preferred_element_type=F32)


def mm_nt(a, b):
    return lax.dot_general(a, b, (((1,), (1,)), ((), ())), preferred_element_type=F32)


def arrived(ref, sem):
    pltpu.make_async_copy(ref, ref, sem).wait()


def cascade_kernel(*refs):
    n_const = 14
    k_hbm, cot_hbm, sens_hbm, index_hbm, first_hbm, second_hbm, b1_ref, b2_ref = refs[:8]
    const_hbm = refs[8 : 8 + n_const]
    pre_hbm, gw_ref = refs[8 + n_const : 10 + n_const]
    rest = refs[10 + n_const :]
    consts = rest[:n_const]
    (
        kv, cv, sv, ksc, ksend, krecv, csc, cs0, cs1, cr0, cr1, pos, ex, hsc,
        img, part, rsrecv, hrecv, tmp, vbuf, hid, act, gp, bcol,
        w1b, w2f, w2b, w1f, agsend, agrecv, regpart, outv, rows_a, rows_b, gsec, ar1, ar2, index_ref, first_ref, second_ref, lines_ref, lines2_ref, wt,
        ld_sem, c_ld, o_sem, k_s, k_r, c_s, c_r, rs_s, rs_r, h_s, h_r, ag_s, ag_r, ar_s, ar_r,
    ) = rest[n_const:]
    (ty, tz, spread, spread_t, pick1, pick2, rowpick, gap1, gap2, gap3, sel_a, sel_b, middle, edge) = consts

    csend, crecv = (cs0, cs1), (cr0, cr1)
    me = lax.axis_index("space")
    co = lax.axis_index("coil")
    hz = co // 2
    hy = co % 2

    load_i = pltpu.make_async_copy(index_hbm, index_ref, ld_sem.at[3])
    load_w = [
        pltpu.make_async_copy(first_hbm, first_ref, ld_sem.at[4]),
        pltpu.make_async_copy(second_hbm, second_ref, ld_sem.at[5]),
    ]
    load_k = pltpu.make_async_copy(k_hbm, kv, ld_sem.at[0])
    load_c = pltpu.make_async_copy(cot_hbm, cv, ld_sem.at[1])
    load_s = pltpu.make_async_copy(sens_hbm, sv, ld_sem.at[2])
    load_i.start()
    load_k.start()

    barrier = pltpu.get_barrier_semaphore()

    def greet(j, _):
        pl.semaphore_signal(
            barrier, inc=1, device_id=(lax.rem(me + j, NS), co), device_id_type=MESH
        )
        return 0

    lax.fori_loop(1, NS, greet, 0, unroll=9)
    for j in range(1, NCOIL):
        pl.semaphore_signal(
            barrier, inc=1, device_id=(me, lax.rem(co + j, NCOIL)), device_id_type=MESH
        )
    row_y, row_zc = me // 16, me % 16
    for jy in range(1, 4):
        for jc in range(1, NCOIL):
            there = (lax.rem(row_y + jy, 4) * 16 + row_zc, lax.rem(co + jc, NCOIL))
            pl.semaphore_signal(barrier, inc=1, device_id=there, device_id_type=MESH)

    load_c.start()
    for load in load_w:
        load.start()
    loads = [
        pltpu.make_async_copy(src, dst, c_ld.at[n])
        for n, (src, dst) in enumerate(zip(const_hbm, consts))
    ]
    for load in loads:
        load.start()
    load_s.start()

    load_i.wait()
    turned = jnp.concatenate(
        [index_ref[...].astype(F32), jnp.full((128 - LINES, NZ), -1.0, F32)], axis=0
    )
    shifted = jnp.concatenate(
        [jnp.full((64, NZ), -1.0, F32), turned[0:64]], axis=0
    )
    late = lax.broadcasted_iota(jnp.int32, (128, NZ), 1) % 4 >= 2
    lines_ref[...] = turned.T.astype(jnp.int32)
    lines2_ref[...] = jnp.where(late, shifted, turned).T.astype(jnp.int32)
    load_k.wait()
    y_rows = lax.broadcasted_iota(jnp.int32, (NY, 128), 0)

    def hot(z):
        row = lines2_ref[pl.ds(me * ZL + z, 1), :]
        return jnp.where(y_rows == row, 1.0, 0.0).astype(BF)

    hots = [hot(z) for z in range(ZL)]
    for p in range(2):
        for zlo in range(2):
            packed = mm(kv[p, :, zlo].reshape(CL * NS, NY), hots[zlo])
            packed += mm(kv[p, :, zlo + 2].reshape(CL * NS, NY), hots[zlo + 2])
            ksc[pl.ds((p * 2 + zlo) * 256, 256), :] = packed

    def pack_k(x, _):
        ksend[x] = ksc[pl.ds(x, 16, stride=NS), :].astype(BF)
        return 0

    lax.fori_loop(0, NS, pack_k, 0, unroll=4)

    def spread_out(src, dst, s_sem, r_sem):
        pltpu.make_async_copy(src.at[me], dst.at[me], r_sem).start()

        def send(j, _):
            to = lax.rem(me + j, NS)
            pltpu.make_async_remote_copy(
                src_ref=src.at[to],
                dst_ref=dst.at[me],
                send_sem=s_sem,
                recv_sem=r_sem,
                device_id=(to, co),
                device_id_type=MESH,
            ).start()
            return 0

        lax.fori_loop(1, NS, send, 0, unroll=3)

    pl.semaphore_wait(barrier, NS - 1 + NCOIL - 1 + 9)
    spread_out(ksend, krecv, k_s, k_r)

    load_c.wait()
    loads[0].wait()

    def cot_y(zl, _):
        rows = mm(cv[0, :, zl].reshape(CL * NS, NY), ty[0:NY])
        rows += mm(cv[1, :, zl].reshape(CL * NS, NY), ty[NY:])
        for j in range(5):
            csc[j, pl.ds(pl.multiple_of(zl * 256, 256), 256), :] = rows[:, j * 128 : (j + 1) * 128]
        return 0

    lax.fori_loop(0, ZL, cot_y, 0)

    def pack_c(x, _):
        for n, (lo, hi) in enumerate(GROUPS):
            for j in range(lo, hi):
                lanes = slice((j - lo) * 128, (j - lo + 1) * 128)
                csend[n][x, :, lanes] = csc[j, pl.ds(x, 16, stride=NS), :].astype(BF)
        return 0

    lax.fori_loop(0, NS, pack_c, 0, unroll=2)

    for n in range(len(GROUPS)):
        spread_out(csend[n], crecv[n], c_s.at[n], c_r.at[n])

    for load in loads[1:]:
        load.wait()
    lane_y = lax.broadcasted_iota(jnp.int32, (32, MR), 1)
    lane_y = jnp.where(lane_y >= NY, lane_y - NY, lane_y)
    upper = jnp.where(lax.broadcasted_iota(jnp.int32, (32, MR), 0) % 4 >= 2, 64, 0)

    def find(g, _):
        rows = pl.ds(pl.multiple_of(g * 32, 32), 32)
        lines = lines_ref[rows, :]
        place = jnp.full((32, MR), 127, jnp.int32)
        for line in range(LINES):
            place = jnp.where(lines[:, line : line + 1] == lane_y, upper + line, place)
        pos[rows, :] = place
        return 0

    lax.fori_loop(0, NZ // 32, find, 0)

    load_s.wait()
    for load in load_w:
        load.wait()

    def to_image(n, j):
        columns = []
        for c in range(CL):
            block = hsc[j, pl.ds(c, NZ, stride=CL), :].T.astype(BF)
            columns.append(jnp.concatenate([block[0:64], block[64:128]], axis=1))
        image = mm(jnp.concatenate(columns, axis=0), tz[...]).astype(BF)
        for c in range(CL):
            img[n, c, j * 64 : (j + 1) * 64, :] = image[c * 64 : (c + 1) * 64]

        def combine(g, _):
            rows = pl.ds(pl.multiple_of(j * 64 + g * 16, 16), 16)
            re = jnp.zeros((16, NZ), F32)
            im = jnp.zeros((16, NZ), F32)
            for c in range(CL):
                both = img[n, c, rows, :].astype(F32)
                i0, i1 = both[:, :NZ], both[:, NZ:]
                s0 = sv[0, c, rows, :].astype(F32)
                s1 = sv[1, c, rows, :].astype(F32)
                re += s0 * i0 + s1 * i1
                im += s0 * i1 - s1 * i0
            if n == 1:
                re, im = -re, -im
            part[n, 0, rows, :] = re.astype(BF)
            part[n, 1, rows, :] = im.astype(BF)
            return 0

        lax.fori_loop(0, 4, combine, 0)

    def coil_send(n, chunk):
        for j, half, row, count, step in PIECES:
            if j != chunk:
                continue
            for half_z in range(2):
                to = half_z * 2 + half
                src = part.at[n, :, pl.ds(row, count), pl.ds(half_z * 128, 128)]
                dst = rsrecv.at[n, co, :, pl.ds(row - half * 144, count)]

                @pl.when(co == to)
                def _():
                    pltpu.make_async_copy(src, dst, rs_r.at[n, step]).start()

                @pl.when(co != to)
                def _():
                    pltpu.make_async_remote_copy(
                        src_ref=src,
                        dst_ref=dst,
                        send_sem=rs_s.at[n, step],
                        recv_sem=rs_r.at[n, step],
                        device_id=(me, to),
                        device_id_type=MESH,
                    ).start()

    def coil_sum(n, step):
        first, count = STEPS[step]
        rows = slice(first, first + count)
        arrived(rsrecv.at[n, :, :, pl.ds(first, count)], rs_r.at[n, step])
        for q in range(2):
            total = rsrecv[n, 0, q, rows].astype(F32)
            for j in range(1, NCOIL):
                total += rsrecv[n, j, q, rows].astype(F32)
            hrecv[n, 4, q, rows] = total.astype(BF)
        for slot, off in enumerate((-2, -1, 1, 2)):
            to = lax.rem(me + off + NS, NS)
            pltpu.make_async_remote_copy(
                src_ref=hrecv.at[n, 4, :, pl.ds(first, count)],
                dst_ref=hrecv.at[n, 3 - slot, :, pl.ds(first, count)],
                send_sem=h_s.at[n, step],
                recv_sem=h_r.at[n, step],
                device_id=(to, co),
                device_id_type=MESH,
            ).start()

    def windows(n, step):
        first, count = STEPS[step]
        arrived(hrecv.at[n, pl.ds(0, 4), :, pl.ds(first, count)], h_r.at[n, step])
        for j, slot in enumerate((0, 1, 4, 2, 3)):
            x = me + j - 2
            inside = jnp.logical_and(x >= 0, x < NS)
            for q in range(2):
                got = hrecv[n, slot, q, first : first + count].astype(F32)
                tmp[j, q, 2 + first : 2 + first + count, :] = jnp.where(inside, got, 0.0)
        for x3 in range(3):
            for blk in range(*BLOCKS[step]):
                lanes = slice((x3 * NB + blk) * 128, (x3 * NB + blk + 1) * 128)
                rows = pl.ds(pl.multiple_of(hy * 16, 16) + blk * BLK, US)
                column = [tmp[x3 + a, q, rows, :] for q in range(2) for a in range(3)]
                vbuf[n, 0 : 6 * US, lanes] = jnp.concatenate(column, axis=0).astype(BF)

    def lanes_of(x3, step):
        lo, hi = BLOCKS[step]
        return slice(x3 * LN + lo * 128, x3 * LN + hi * 128)

    def into_hidden(n, w, step):
        for x3 in range(3):
            lanes = lanes_of(x3, step)
            hid[n, :, lanes] = mm(w[...], vbuf[n, :, lanes])

    x_ok = [jnp.logical_and(me + d >= 0, me + d < NS) for d in (-1, 0, 1)]

    def keep(value, kind, x3, blk):
        if blk == 0:
            value = jnp.where(jnp.logical_and(kind == 1.0, hy == 0), 0.0, value)
        if blk == NB - 1:
            value = jnp.where(jnp.logical_and(kind == 2.0, hy == 1), 0.0, value)
        if x3 != 1:
            value = jnp.where(x_ok[x3], value, 0.0)
        return value

    def out_of_hidden(values, w, step):
        total = mm(w[0], values[:, lanes_of(0, step)])
        total += mm(w[1], values[:, lanes_of(1, step)])
        total += mm(w[2], values[:, lanes_of(2, step)])
        return total

    def gather_send(n, step):
        lo, hi = BLOCKS[step]
        rows = pl.ds(lo * BLK, (hi - lo) * BLK)
        src = agsend.at[n, :, rows]
        dst = agrecv.at[n, co, :, rows]
        pltpu.make_async_copy(src, dst, ag_r.at[n, step]).start()
        for j in range(1, NCOIL):
            to = lax.rem(co + j, NCOIL)
            pltpu.make_async_remote_copy(
                src_ref=src,
                dst_ref=dst,
                send_sem=ag_s.at[n, step],
                recv_sem=ag_r.at[n, step],
                device_id=(me, to),
                device_id_type=MESH,
            ).start()

    def gathered(n):
        for step, (lo, hi) in enumerate(BLOCKS):
            arrived(agrecv.at[n, :, :, pl.ds(lo * BLK, (hi - lo) * BLK)], ag_r.at[n, step])

    def second_grad():
        rows_b[...] = jnp.zeros((24, MR), F32)
        own = jnp.concatenate(
            [
                jnp.concatenate(
                    [
                        hrecv[1, 4, q, pl.ds(pl.multiple_of(hy * 16, 16) + blk * BLK, BLK), :]
                        for blk in range(NB)
                    ],
                    axis=1,
                )
                for q in range(2)
            ],
            axis=0,
        )
        for a in range(3):
            cross = mm_nt(own, act[:, a * LN : (a + 1) * LN])
            for q in range(2):
                rows = slice(q * BLK, (q + 1) * BLK)
                for b in range(3):
                    at = a * 6 + b * 2 + q
                    rows_b[at : at + 1, :] = jnp.sum(
                        jnp.where(gap2[rows, :] == float(b), cross[rows, :], 0.0),
                        axis=0,
                        keepdims=True,
                    )
        high = lax.Precision.HIGHEST
        grads = jnp.dot(rows_b[...], sel_b[...], precision=high, preferred_element_type=F32)
        at_row = lax.broadcasted_iota(jnp.int32, (24, 128), 0)
        at_lane = lax.broadcasted_iota(jnp.int32, (24, 128), 1)
        own_f = own.astype(F32)
        for q in range(2):
            spot = jnp.logical_and(at_row == 18, at_lane == CH + q)
            grads += jnp.where(spot, jnp.sum(own_f[q * BLK : (q + 1) * BLK]), 0.0)
        gsec[...] = grads

    arrived(krecv, k_r)
    low_rows = lax.broadcasted_iota(jnp.int32, (8, MR), 0) < 4
    low_lanes = lax.broadcasted_iota(jnp.int32, (8, 128), 1) < 64

    def pick(values, index):
        return jnp.take_along_axis(values, index, axis=1, mode="promise_in_bounds")

    def expand(s, _):
        got = krecv[s].astype(F32)
        halves = []
        for zhi in range(2):
            first = pos[pl.ds(s * 4 + 2 * zhi, 1), :]
            second = pos[pl.ds(s * 4 + 2 * zhi + 1, 1), :]
            index = jnp.where(
                low_rows,
                jnp.broadcast_to(first, (8, MR)),
                jnp.broadcast_to(second, (8, MR)),
            )
            at = [index[:, j * 128 : (j + 1) * 128] for j in range(5)]
            re, im = got[0:8], got[8:16]
            halves.append(
                jnp.concatenate(
                    [
                        pick(re, at[0]),
                        pick(re, at[1]),
                        jnp.where(low_lanes, pick(re, at[2]), pick(im, at[2])),
                        pick(im, at[3]),
                        pick(im, at[4]),
                    ],
                    axis=1,
                )
            )
        ex[pl.ds(pl.multiple_of(s * 16, 16), 16), :] = jnp.concatenate(halves, axis=0).astype(BF)
        return 0

    lax.fori_loop(0, NS, expand, 0, unroll=8)

    def k_y(g, _):
        rows = pl.ds(pl.multiple_of(g * 256, 256), 256)
        half = mm(ex[rows, :], ty[...]).astype(BF).astype(F32)
        for j in range(5):
            hsc[j, rows, :] = half[:, j * 128 : (j + 1) * 128]
        return 0

    lax.fori_loop(0, 4, k_y, 0)
    for j in range(NCH):
        to_image(0, j)
        coil_send(0, j)

    def take_cot(n):
        lo, hi = GROUPS[n]
        arrived(crecv[n], c_r.at[n])
        for j in range(lo, hi):
            lanes = slice((j - lo) * 128, (j - lo + 1) * 128)
            hsc[j] = crecv[n][:, :, lanes].astype(F32).reshape(16 * NS, 128)
            to_image(1, j)
            coil_send(1, j)

    wt[...] = jnp.zeros((2, 128, 128), F32)
    for n, ref in enumerate((first_ref, second_ref)):
        for a in range(3):
            for b in range(3):
                at = (a * 3 + b) * 2
                wt[n, at : at + 2, 0:CH] = ref[a, b].astype(F32)
    w1 = wt[0].astype(BF)
    w2 = wt[1].astype(BF)
    sp = spread[...]
    spt = spread_t[...]
    by_hidden1 = mm_nt(sp, w1).astype(BF)
    by_hidden2 = mm_nt(sp, w2).astype(BF)
    band1 = jnp.zeros((MR, KR), F32)
    band2 = jnp.zeros((MR, KR), F32)
    for b in range(3):
        hit = gap1[...] == float(b)
        band1 += jnp.where(hit, mm(by_hidden1, pick1[b]), 0.0)
        band2 += jnp.where(hit, mm(by_hidden2, pick2[b]), 0.0)
    w1b[...] = band1.astype(BF)
    w2f[...] = band2.astype(BF)
    for a in range(3):
        out2 = jnp.zeros((64, MR), F32)
        out1 = jnp.zeros((64, MR), F32)
        for b in range(3):
            hit = gap2[...] == float(b)
            out2 += jnp.where(hit, mm(mm(rowpick[a * 3 + b], w2).astype(BF), spt), 0.0)
            flipped = rowpick[(2 - a) * 3 + (2 - b)]
            out1 += jnp.where(hit, mm(mm(flipped, w1).astype(BF), spt), 0.0)
        w2b[a] = out2.astype(BF)
        w1f[a] = out1.astype(BF)
    lane = lax.broadcasted_iota(jnp.int32, (1, 128), 1)
    row = jnp.zeros((1, 128), F32)
    for ch in range(CH):
        row = jnp.where(lane == ch, b1_ref[ch], row)
    bias = jnp.sum(sp.astype(F32) * row, axis=1, keepdims=True)
    bcol[...] = jnp.broadcast_to(bias, (MR, 128))
    zero_rows = jnp.zeros((KR - 6 * US, 3 * LN), BF)
    for n in range(2):
        vbuf[n, 6 * US :, :] = zero_rows
    for j in range(5):
        for i in range(2):
            tmp[j, i, 0:8, :] = jnp.zeros((8, 128), F32)
            tmp[j, i, 176:TR, :] = jnp.zeros((TR - 176, 128), F32)

    coil_sum(0, 0)
    coil_sum(0, 1)
    take_cot(0)
    take_cot(1)
    coil_sum(1, 0)
    for step in range(2):
        windows(0, step)
        into_hidden(0, w1b, step)

    def activate(g, _):
        rows = pl.ds(pl.multiple_of(g * 16, 16), 16)
        kind = edge[rows, :]
        add = bcol[rows, :]
        for x3 in range(3):
            for blk in range(NB):
                lanes = slice((x3 * NB + blk) * 128, (x3 * NB + blk + 1) * 128)
                h = hid[0, rows, lanes] + add
                s = 0.5 * jnp.tanh(0.5 * h) + 0.5
                act[rows, lanes] = keep(h * s, kind, x3, blk).astype(BF)
                hid[0, rows, lanes] = s * (1.0 + h * (1.0 - s))
        return 0

    lax.fori_loop(0, MR // 16, activate, 0)
    for step, (lo, hi) in enumerate(BLOCKS):
        regularized = out_of_hidden(act, w2b, step)
        for q in range(2):
            for blk in range(lo, hi):
                lanes = slice((blk - lo) * 128, (blk - lo + 1) * 128)
                block = regularized[q * BLK : (q + 1) * BLK, lanes] + b2_ref[q]
                agsend[0, q, blk * BLK : (blk + 1) * BLK, :] = block.astype(BF)
        gather_send(0, step)

    coil_sum(1, 1)
    second_grad()

    def grad_blocks(step):
        lo, hi = BLOCKS[step]
        windows(1, step)
        into_hidden(1, w2f, step)

        def grad_hidden(g, _):
            rows = pl.ds(pl.multiple_of(g * 16, 16), 16)
            kind = edge[rows, :]
            for x3 in range(3):
                for blk in range(lo, hi):
                    lanes = slice((x3 * NB + blk) * 128, (x3 * NB + blk + 1) * 128)
                    value = hid[1, rows, lanes] * hid[0, rows, lanes]
                    gp[rows, lanes] = keep(value, kind, x3, blk).astype(BF)
            return 0

        lax.fori_loop(0, MR // 16, grad_hidden, 0, unroll=2)
        grad_comb = out_of_hidden(gp, w1f, step)
        for q in range(2):
            for blk in range(lo, hi):
                lanes = slice((blk - lo) * 128, (blk - lo + 1) * 128)
                block = grad_comb[q * BLK : (q + 1) * BLK, lanes]
                agsend[1, q, blk * BLK : (blk + 1) * BLK, :] = block.astype(BF)
        gather_send(1, step)

    grad_blocks(0)
    grad_blocks(1)

    gathered(0)

    def quarters(g):
        for half_y in range(2):
            for half_z in range(2):
                src = pl.ds(pl.multiple_of(g * 16, 16), 16)
                dst = pl.ds(pl.multiple_of(half_y * 160 + g * 16, 16), 16)
                lo = slice(half_z * 128, half_z * 128 + 128)
                hi = slice(NZ + half_z * 128, NZ + half_z * 128 + 128)
                yield half_z * 2 + half_y, src, dst, lo, hi

    def begin(g, _):
        for slot, src, dst, lo, hi in quarters(g):
            r0 = agrecv[0, slot, 0, src, :].astype(F32)
            r1 = agrecv[0, slot, 1, src, :].astype(F32)
            for c in range(CL):
                k0 = img[1, c, dst, lo].astype(F32)
                k1 = img[1, c, dst, hi].astype(F32)
                regpart[0, c, dst, lo] = k0 * r0 + k1 * r1
                regpart[1, c, dst, lo] = k1 * r0 - k0 * r1
        return 0

    rows_a[...] = jnp.zeros((24, MR), F32)
    gp_mid = gp[:, LN : 2 * LN]
    cross = mm_nt(vbuf[0, :, LN : 2 * LN], gp_mid)
    for i in range(2):
        for a in range(3):
            rows = slice((i * 3 + a) * US, (i * 3 + a + 1) * US)
            block = cross[rows, :]
            gap = gap3[rows, :]
            for b in range(3):
                at = (a * 3 + b) * 2 + i
                rows_a[at : at + 1, :] = jnp.sum(
                    jnp.where(gap == float(b), block, 0.0), axis=0, keepdims=True
                )
    sums = mm_nt(jnp.ones((8, LN), BF), gp_mid) * middle[...]
    rows_a[18:19, :] = sums[0:1, :]
    high = lax.Precision.HIGHEST
    grads = jnp.dot(rows_a[...], sel_a[...], precision=high, preferred_element_type=F32)
    grads += gsec[...]
    def share(n, buf, count, mine, device):
        buf[mine] = grads_in[n]
        for j in range(1, count):
            to = lax.rem(mine + j, count)
            pltpu.make_async_remote_copy(
                src_ref=buf.at[mine],
                dst_ref=buf.at[mine],
                send_sem=ar_s.at[n],
                recv_sem=ar_r.at[n],
                device_id=device(to),
                device_id_type=MESH,
            ).start()

    def collect(n, buf, count):
        arrived(buf.at[pl.ds(0, count - 1)], ar_r.at[n])
        total = buf[0]
        for j in range(1, count):
            total += buf[j]
        return total

    grads = grads[0:8] + pltpu.roll(grads[8:16], 36, 1) + pltpu.roll(grads[16:24], 72, 1)
    grads_in = [grads]
    share(0, ar1, 16, row_zc, lambda to: (row_y * 16 + to, co))

    lax.fori_loop(0, 10, begin, 0)
    grads_in.append(collect(0, ar1, 16))
    share(1, ar2, 16, row_y * 4 + co, lambda to: (to // 4 * 16 + row_zc, to % 4))
    gathered(1)

    def result(half):
        def finish(g, _):
            for slot, src, dst, lo, hi in quarters(g):
                g0 = agrecv[1, slot, 0, src, :].astype(F32)
                g1 = agrecv[1, slot, 1, src, :].astype(F32)
                for c in range(half * 2, half * 2 + 2):
                    i0 = img[0, c, dst, lo].astype(F32)
                    i1 = img[0, c, dst, hi].astype(F32)
                    re = i0 * g0 + i1 * g1 - regpart[0, c, dst, lo]
                    im = i1 * g0 - i0 * g1 - regpart[1, c, dst, lo]
                    outv[0, c, dst, lo] = re.astype(BF)
                    outv[1, c, dst, lo] = im.astype(BF)
            return 0

        lax.fori_loop(0, 10, finish, 0)
        for p in range(2):
            store(p, half).start()

    def store(p, half):
        coils = pl.ds(half * 2, 2)
        return pltpu.make_async_copy(
            outv.at[p, coils], pre_hbm.at[p, coils], o_sem.at[p * 2 + half]
        )

    result(0)

    result(1)
    gw_ref[...] = collect(1, ar2, 16) * (1.0 / math.sqrt(NS * NY * NZ))

    arrived(ksend.at[pl.ds(0, NS - 1)], k_s)
    for n in range(len(GROUPS)):
        arrived(csend[n].at[pl.ds(0, NS - 1)], c_s.at[n])
    for n in range(2):
        for step, (first, count) in enumerate(STEPS):
            arrived(rsrecv.at[n, pl.ds(0, 3), :, pl.ds(first, count)], rs_s.at[n, step])
            arrived(hrecv.at[n, pl.ds(0, 4), :, pl.ds(first, count)], h_s.at[n, step])
        for step, (lo, hi) in enumerate(BLOCKS):
            piece = agrecv.at[n, pl.ds(0, NCOIL - 1), :, pl.ds(lo * BLK, (hi - lo) * BLK)]
            arrived(piece, ag_s.at[n, step])
    arrived(ar1.at[pl.ds(0, 15)], ar_s.at[0])
    arrived(ar2.at[pl.ds(0, 15)], ar_s.at[1])
    for p in range(2):
        for half in range(2):
            store(p, half).wait()


def final_kernel(pre_hbm, gw_hbm, out_hbm, g1_hbm, gb1_hbm, g2_hbm, gb2_hbm, *scratch):
    held, folded_ref, g1_ref, gb1_ref, g2_ref, gb2_ref, sem_in, sem_out, sem_small = scratch
    load_g = pltpu.make_async_copy(gw_hbm, folded_ref, sem_small.at[4])
    load_g.start()
    spots = [(p, c) for p in range(2) for c in range(CL)]
    loads = [pltpu.make_async_copy(pre_hbm.at[s], held.at[s], sem_in.at[s]) for s in spots]
    stores = [pltpu.make_async_copy(held.at[s], out_hbm.at[s], sem_out.at[s]) for s in spots]
    for load in loads:
        load.start()
    load_g.wait()
    folded = folded_ref[...]
    first = jnp.concatenate([folded, pltpu.roll(folded, 92, 1), pltpu.roll(folded, 56, 1)], axis=0)
    second = pltpu.roll(first, 128 - CH, 1)
    for a in range(3):
        for b in range(3):
            at = (a * 3 + b) * 2
            g1_ref[a, b] = first[at : at + 2, 0:CH]
            g2_ref[a, b] = second[at : at + 2, 0:CH]
    gb1_ref[...] = first[18:19, 0:CH]
    gb2_ref[...] = second[18:19, 0:2]
    small = [(g1_ref, g1_hbm), (gb1_ref, gb1_hbm), (g2_ref, g2_hbm), (gb2_ref, gb2_hbm)]
    stores += [pltpu.make_async_copy(*pair, sem_small.at[n]) for n, pair in enumerate(small)]
    for store in stores[8:]:
        store.start()
    for load, store in zip(loads, stores):
        load.wait()
        store.start()
    for store in stores:
        store.wait()


def on_device(k_space, cotangent, sens_maps, line_index, w_first, b_first, w_second, b_second):
    constants = make_constants()
    sens = jnp.transpose(sens_maps.reshape(2, CL, NZ, NY), (0, 1, 3, 2))
    index = jnp.transpose(line_index)
    first = jnp.transpose(w_first, (2, 3, 1, 0))
    second = jnp.transpose(w_second, (2, 3, 0, 1))
    vm = pl.BlockSpec(memory_space=pltpu.VMEM)
    anym = pl.BlockSpec(memory_space=pl.ANY)
    dma = pltpu.SemaphoreType.DMA
    scratch = [pltpu.VMEM(c.shape, c.dtype) for c in constants]
    scratch += [
        pltpu.VMEM((2, CL, ZL, NS, NY), BF),
        pltpu.VMEM((2, CL, ZL, NS, NY), BF),
        pltpu.VMEM((2, CL, NY, NZ), BF),
        pltpu.VMEM((16 * NS, 128), F32),
        pltpu.VMEM((NS, 16, 128), BF),
        pltpu.VMEM((NS, 16, 128), BF),
        pltpu.VMEM((5, 16 * NS, 128), F32),
        *[pltpu.VMEM((NS, 16, 128 * (hi - lo)), BF) for lo, hi in GROUPS],
        *[pltpu.VMEM((NS, 16, 128 * (hi - lo)), BF) for lo, hi in GROUPS],
        pltpu.VMEM((NZ, 640), jnp.int32),
        pltpu.VMEM((NZ * CL, 640), BF),
        pltpu.VMEM((5, NZ * CL, 128), F32),
        pltpu.VMEM((2, CL, NY, 2 * NZ), BF),
        pltpu.VMEM((2, 2, NY, NZ), BF),
        pltpu.VMEM((2, NCOIL, 2, PR, 128), BF),
        pltpu.VMEM((2, 5, 2, PR, 128), BF),
        pltpu.VMEM((5, 2, TR, 128), F32),
        pltpu.VMEM((2, KR, 3 * LN), BF),
        pltpu.VMEM((2, MR, 3 * LN), F32),
        pltpu.VMEM((MR, 3 * LN), BF),
        pltpu.VMEM((MR, 3 * LN), BF),
        pltpu.VMEM((MR, 128), F32),
        pltpu.VMEM((MR, KR), BF),
        pltpu.VMEM((MR, KR), BF),
        pltpu.VMEM((3, 64, MR), BF),
        pltpu.VMEM((3, 64, MR), BF),
        pltpu.VMEM((2, 2, NY // 2, 128), BF),
        pltpu.VMEM((2, NCOIL, 2, NY // 2, 128), BF),
        pltpu.VMEM((2, CL, NY, NZ), F32),
        pltpu.VMEM((2, CL, NY, NZ), BF),
        pltpu.VMEM((24, MR), F32),
        pltpu.VMEM((24, MR), F32),
        pltpu.VMEM((24, 128), F32),
        pltpu.VMEM((16, 8, 128), F32),
        pltpu.VMEM((16, 8, 128), F32),
        pltpu.VMEM((LINES, NZ), jnp.int32),
        pltpu.VMEM((3, 3, 2, CH), BF),
        pltpu.VMEM((3, 3, 2, CH), BF),
        pltpu.VMEM((NZ, 128), jnp.int32),
        pltpu.VMEM((NZ, 128), jnp.int32),
        pltpu.VMEM((2, 128, 128), F32),
        dma((6,)),
        dma((len(constants),)),
        dma((4,)),
        dma,
        dma,
        dma((len(GROUPS),)),
        dma((len(GROUPS),)),
        dma((2, 2)),
        dma((2, 2)),
        dma((2, 2)),
        dma((2, 2)),
        dma((2, 2)),
        dma((2, 2)),
        dma((2,)),
        dma((2,)),
    ]
    smem = pl.BlockSpec(memory_space=pltpu.SMEM)
    result, grads = pl.pallas_call(
        cascade_kernel,
        out_shape=(
            jax.ShapeDtypeStruct((2, CL, NY, NZ), BF),
            jax.ShapeDtypeStruct((8, 128), F32),
        ),
        in_specs=[anym] * 6 + [smem] * 2 + [anym] * len(constants),
        out_specs=(anym, vm),
        scratch_shapes=scratch,
        compiler_params=pltpu.CompilerParams(
            collective_id=0, has_side_effects=True, vmem_limit_bytes=60 * 1024 * 1024
        ),
    )(k_space, cotangent, sens, index, first, second, b_first, b_second, *constants)
    grad_sens, grad_w1, grad_b1, grad_w2, grad_b2 = pl.pallas_call(
        final_kernel,
        out_shape=(
            jax.ShapeDtypeStruct((2, CL, NY, NZ), BF),
            jax.ShapeDtypeStruct((3, 3, 2, CH), F32),
            jax.ShapeDtypeStruct((1, CH), F32),
            jax.ShapeDtypeStruct((3, 3, 2, CH), F32),
            jax.ShapeDtypeStruct((1, 2), F32),
        ),
        in_specs=[anym] * 2,
        out_specs=(anym,) * 5,
        scratch_shapes=[
            pltpu.VMEM((2, CL, NY, NZ), BF),
            pltpu.VMEM((8, 128), F32),
            pltpu.VMEM((3, 3, 2, CH), F32),
            pltpu.VMEM((1, CH), F32),
            pltpu.VMEM((3, 3, 2, CH), F32),
            pltpu.VMEM((1, 2), F32),
            dma((2, CL)),
            dma((2, CL)),
            dma((5,)),
        ],
        compiler_params=pltpu.CompilerParams(vmem_limit_bytes=60 * 1024 * 1024),
    )(result, grads)
    grad_sens = jnp.transpose(grad_sens, (0, 1, 3, 2)).reshape(2, CL, NZ, 1, NY)
    grad_w1 = jnp.transpose(grad_w1, (3, 2, 0, 1))
    grad_w2 = jnp.transpose(grad_w2, (2, 3, 0, 1))
    grad_b1 = grad_b1.reshape(CH)
    grad_b2 = grad_b2.reshape(2)
    return (grad_sens, grad_w1, grad_b1, grad_w2, grad_b2)


def solution(mesh):
    placed = (
        P(None, "coil", "space", None, None),
        P(None, "coil", "space", None, None),
        P(None, "coil", None, "space", None),
        P(),
        P(),
        P(),
        P(),
        P(),
    )
    return jax.shard_map(
        on_device,
        mesh=mesh,
        in_specs=placed,
        out_specs=(P(None, "coil", None, "space", None), P(), P(), P(), P()),
        check_vma=False,
    )
```

```python
import math

import jax
import jax.numpy as jnp
import numpy as np
import ml_dtypes
from jax import lax
from jax.experimental import pallas as pl
from jax.experimental.pallas import tpu as pltpu
from jax.sharding import PartitionSpec as P

MESH = pl.DeviceIdType.MESH
BF = jnp.bfloat16
F32 = jnp.float32
NS, NCOIL = 64, 4
NY, NZ, CH, LINES = 320, 256, 18, 40
CL, ZL = 4, 4
BLK, NB = 32, 5
HV, HU, US = 34, 36, 40
MR, KR = 640, 256
PR = 176
TR = 192
LN = NB * 128
NCH = 5
GROUPS = ((0, 4), (4, 5))
PIECES = (
    (0, 0, 0, 64, 0),
    (1, 0, 64, 48, 0),
    (1, 0, 112, 16, 1),
    (2, 0, 128, 48, 1),
    (2, 1, 144, 48, 0),
    (3, 1, 192, 64, 0),
    (4, 1, 256, 64, 1),
)
BLOCKS = ((0, 2), (2, 5))
STEPS = ((0, 112), (112, 64))


def one_hot(rows, cols, pairs):
    table = np.zeros((rows, cols), np.float32)
    for r, c in pairs:
        table[r, c] = 1.0
    return table


def dft_matrix(length):
    position = np.arange(length)
    angles = 2.0 * math.pi / length * ((position[:, None] * position[None, :]) % length)
    cosine = np.cos(angles) / math.sqrt(length)
    sine = np.sin(angles) / math.sqrt(length)
    return np.block([[cosine, sine], [-sine, cosine]]).astype(ml_dtypes.bfloat16)


def make_constants():
    bf = ml_dtypes.bfloat16
    table_y = dft_matrix(NY).reshape(2 * NY, 2, NCH, 64)
    table_y = np.ascontiguousarray(table_y.transpose(0, 2, 1, 3)).reshape(2 * NY, 2 * NY)
    hid = [(ch * HV + v, ch, v) for ch in range(CH) for v in range(HV)]
    inp = [((i * 3 + a) * US + u, i, a, u) for i in range(2) for a in range(3) for u in range(HU)]
    spread = one_hot(MR, 128, [(r, ch) for r, ch, _ in hid])
    pick1 = np.stack(
        [one_hot(128, KR, [((a * 3 + b) * 2 + i, r) for r, i, a, _ in inp]) for b in range(3)]
    )
    pick2 = np.stack(
        [
            one_hot(128, KR, [((8 - a * 3 - b) * 2 + i, r) for r, i, a, _ in inp])
            for b in range(3)
        ]
    )
    rowpick = np.stack(
        [
            one_hot(
                64, 128, [(q * BLK + t, (a * 3 + b) * 2 + q) for q in range(2) for t in range(BLK)]
            )
            for a in range(3)
            for b in range(3)
        ]
    )
    gap1 = np.full((MR, KR), 99.0, np.float32)
    for r, _, v in hid:
        for s, _, _, u in inp:
            gap1[r, s] = u - v
    gap2 = np.full((64, MR), 99.0, np.float32)
    for q in range(2):
        for t in range(BLK):
            for r, _, v in hid:
                gap2[q * BLK + t, r] = v - t
    inner = np.zeros((MR,), bool)
    for r, _, v in hid:
        inner[r] = 1 <= v <= BLK
    gap3 = np.where(inner[None, :], gap1.T, 99.0).astype(np.float32)
    middle = np.broadcast_to(inner[None, :], (8, MR)).astype(np.float32)
    edge = np.zeros((MR, 128), np.float32)
    for r, _, v in hid:
        edge[r] = 1.0 if v == 0 else 2.0 if v == HV - 1 else 0.0
    return [
        table_y,
        dft_matrix(NZ),
        spread.astype(bf),
        np.ascontiguousarray(spread.T).astype(bf),
        pick1.astype(bf),
        pick2.astype(bf),
        rowpick.astype(bf),
        gap1,
        gap2,
        gap3,
        middle,
        edge,
    ]


def mm(a, b):
    return jnp.dot(a, b, preferred_element_type=F32)


def mm_nt(a, b):
    return lax.dot_general(a, b, (((1,), (1,)), ((), ())), preferred_element_type=F32)


def arrived(ref, sem):
    pltpu.make_async_copy(ref, ref, sem).wait()


def cascade_kernel(*refs):
    n_const = 12
    k_hbm, cot_hbm, sens_hbm, index_hbm, first_hbm, second_hbm, b1_ref, b2_ref = refs[:8]
    const_hbm = refs[8 : 8 + n_const]
    pre_hbm, gw_ref = refs[8 + n_const : 10 + n_const]
    rest = refs[10 + n_const :]
    consts = rest[:n_const]
    (
        kv, cv, sv, ksc, ksend, krecv, csc, cs0, cs1, cr0, cr1, pos, ex, hsc,
        img, part, rsrecv, hrecv, tmp, vbuf, hid, act, gp, bcol,
        w1b, w2f, w2b, w1f, agsend, agrecv, regpart, outv, rows_a, rows_b, gsec, ar1, ar2, index_ref, first_ref, second_ref, lines_ref, lines2_ref, wt,
        ld_sem, c_ld, o_sem, k_s, k_r, c_s, c_r, rs_s, rs_r, h_s, h_r, ag_s, ag_r, ar_s, ar_r,
    ) = rest[n_const:]
    (ty, tz, spread, spread_t, pick1, pick2, rowpick, gap1, gap2, gap3, middle, edge) = consts

    csend, crecv = (cs0, cs1), (cr0, cr1)
    me = lax.axis_index("space")
    co = lax.axis_index("coil")
    hz = co // 2
    hy = co % 2

    load_i = pltpu.make_async_copy(index_hbm, index_ref, ld_sem.at[3])
    load_w = [
        pltpu.make_async_copy(first_hbm, first_ref, ld_sem.at[4]),
        pltpu.make_async_copy(second_hbm, second_ref, ld_sem.at[5]),
    ]
    load_k = pltpu.make_async_copy(k_hbm, kv, ld_sem.at[0])
    load_c = pltpu.make_async_copy(cot_hbm, cv, ld_sem.at[1])
    load_s = pltpu.make_async_copy(sens_hbm, sv, ld_sem.at[2])
    load_i.start()
    load_k.start()

    barrier = pltpu.get_barrier_semaphore()

    def greet(j, _):
        pl.semaphore_signal(
            barrier, inc=1, device_id=(lax.rem(me + j, NS), co), device_id_type=MESH
        )
        return 0

    lax.fori_loop(1, NS, greet, 0, unroll=9)
    for j in range(1, NCOIL):
        pl.semaphore_signal(
            barrier, inc=1, device_id=(me, lax.rem(co + j, NCOIL)), device_id_type=MESH
        )
    row_y, row_zc = me // 16, me % 16
    for jy in range(1, 4):
        for jc in range(1, NCOIL):
            there = (lax.rem(row_y + jy, 4) * 16 + row_zc, lax.rem(co + jc, NCOIL))
            pl.semaphore_signal(barrier, inc=1, device_id=there, device_id_type=MESH)

    load_c.start()
    for load in load_w:
        load.start()
    loads = [
        pltpu.make_async_copy(src, dst, c_ld.at[n])
        for n, (src, dst) in enumerate(zip(const_hbm, consts))
    ]
    for load in loads:
        load.start()
    load_s.start()

    load_i.wait()
    turned = jnp.concatenate(
        [index_ref[...].astype(F32), jnp.full((128 - LINES, NZ), -1.0, F32)], axis=0
    )
    shifted = jnp.concatenate(
        [jnp.full((64, NZ), -1.0, F32), turned[0:64]], axis=0
    )
    late = lax.broadcasted_iota(jnp.int32, (128, NZ), 1) % 4 >= 2
    lines_ref[...] = turned.T.astype(jnp.int32)
    lines2_ref[...] = jnp.where(late, shifted, turned).T.astype(jnp.int32)
    load_k.wait()
    y_rows = lax.broadcasted_iota(jnp.int32, (NY, 128), 0)

    def hot(z):
        row = lines2_ref[pl.ds(me * ZL + z, 1), :]
        return jnp.where(y_rows == row, 1.0, 0.0).astype(BF)

    hots = [hot(z) for z in range(ZL)]
    for p in range(2):
        for zlo in range(2):
            packed = mm(kv[p, :, zlo].reshape(CL * NS, NY), hots[zlo])
            packed += mm(kv[p, :, zlo + 2].reshape(CL * NS, NY), hots[zlo + 2])
            ksc[pl.ds((p * 2 + zlo) * 256, 256), :] = packed

    def pack_k(x, _):
        ksend[x] = ksc[pl.ds(x, 16, stride=NS), :].astype(BF)
        return 0

    lax.fori_loop(0, NS, pack_k, 0, unroll=4)

    def spread_out(src, dst, s_sem, r_sem):
        pltpu.make_async_copy(src.at[me], dst.at[me], r_sem).start()

        def send(j, _):
            to = lax.rem(me + j, NS)
            pltpu.make_async_remote_copy(
                src_ref=src.at[to],
                dst_ref=dst.at[me],
                send_sem=s_sem,
                recv_sem=r_sem,
                device_id=(to, co),
                device_id_type=MESH,
            ).start()
            return 0

        lax.fori_loop(1, NS, send, 0, unroll=3)

    pl.semaphore_wait(barrier, NS - 1 + NCOIL - 1 + 9)
    spread_out(ksend, krecv, k_s, k_r)

    load_c.wait()
    loads[0].wait()

    def cot_y(zl, _):
        rows = mm(cv[0, :, zl].reshape(CL * NS, NY), ty[0:NY])
        rows += mm(cv[1, :, zl].reshape(CL * NS, NY), ty[NY:])
        for j in range(5):
            csc[j, pl.ds(pl.multiple_of(zl * 256, 256), 256), :] = rows[:, j * 128 : (j + 1) * 128]
        return 0

    lax.fori_loop(0, ZL, cot_y, 0)

    def pack_c(x, _):
        for n, (lo, hi) in enumerate(GROUPS):
            for j in range(lo, hi):
                lanes = slice((j - lo) * 128, (j - lo + 1) * 128)
                csend[n][x, :, lanes] = csc[j, pl.ds(x, 16, stride=NS), :].astype(BF)
        return 0

    lax.fori_loop(0, NS, pack_c, 0, unroll=2)

    for n in range(len(GROUPS)):
        spread_out(csend[n], crecv[n], c_s.at[n], c_r.at[n])

    for load in loads[1:]:
        load.wait()
    lane_y = lax.broadcasted_iota(jnp.int32, (32, MR), 1)
    lane_y = jnp.where(lane_y >= NY, lane_y - NY, lane_y)
    upper = jnp.where(lax.broadcasted_iota(jnp.int32, (32, MR), 0) % 4 >= 2, 64, 0)

    def find(g, _):
        rows = pl.ds(pl.multiple_of(g * 32, 32), 32)
        lines = lines_ref[rows, :]
        place = jnp.full((32, MR), 127, jnp.int32)
        for line in range(LINES):
            place = jnp.where(lines[:, line : line + 1] == lane_y, upper + line, place)
        pos[rows, :] = place
        return 0

    lax.fori_loop(0, NZ // 32, find, 0)

    load_s.wait()
    for load in load_w:
        load.wait()

    def to_image(n, j):
        columns = []
        for c in range(CL):
            block = hsc[j, pl.ds(c, NZ, stride=CL), :].T.astype(BF)
            columns.append(jnp.concatenate([block[0:64], block[64:128]], axis=1))
        image = mm(jnp.concatenate(columns, axis=0), tz[...]).astype(BF)
        for c in range(CL):
            img[n, c, j * 64 : (j + 1) * 64, :] = image[c * 64 : (c + 1) * 64]

        def combine(g, _):
            rows = pl.ds(pl.multiple_of(j * 64 + g * 16, 16), 16)
            re = jnp.zeros((16, NZ), F32)
            im = jnp.zeros((16, NZ), F32)
            for c in range(CL):
                both = img[n, c, rows, :].astype(F32)
                i0, i1 = both[:, :NZ], both[:, NZ:]
                s0 = sv[0, c, rows, :].astype(F32)
                s1 = sv[1, c, rows, :].astype(F32)
                re += s0 * i0 + s1 * i1
                im += s0 * i1 - s1 * i0
            if n == 1:
                re, im = -re, -im
            part[n, 0, rows, :] = re.astype(BF)
            part[n, 1, rows, :] = im.astype(BF)
            return 0

        lax.fori_loop(0, 4, combine, 0)

    def coil_send(n, chunk):
        for j, half, row, count, step in PIECES:
            if j != chunk:
                continue
            for half_z in range(2):
                to = half_z * 2 + half
                src = part.at[n, :, pl.ds(row, count), pl.ds(half_z * 128, 128)]
                dst = rsrecv.at[n, co, :, pl.ds(row - half * 144, count)]

                @pl.when(co == to)
                def _():
                    pltpu.make_async_copy(src, dst, rs_r.at[n, step]).start()

                @pl.when(co != to)
                def _():
                    pltpu.make_async_remote_copy(
                        src_ref=src,
                        dst_ref=dst,
                        send_sem=rs_s.at[n, step],
                        recv_sem=rs_r.at[n, step],
                        device_id=(me, to),
                        device_id_type=MESH,
                    ).start()

    def coil_sum(n, step):
        first, count = STEPS[step]
        rows = slice(first, first + count)
        arrived(rsrecv.at[n, :, :, pl.ds(first, count)], rs_r.at[n, step])
        for q in range(2):
            total = rsrecv[n, 0, q, rows].astype(F32)
            for j in range(1, NCOIL):
                total += rsrecv[n, j, q, rows].astype(F32)
            hrecv[n, 4, q, rows] = total.astype(BF)
        for slot, off in enumerate((-2, -1, 1, 2)):
            to = lax.rem(me + off + NS, NS)
            pltpu.make_async_remote_copy(
                src_ref=hrecv.at[n, 4, :, pl.ds(first, count)],
                dst_ref=hrecv.at[n, 3 - slot, :, pl.ds(first, count)],
                send_sem=h_s.at[n, step],
                recv_sem=h_r.at[n, step],
                device_id=(to, co),
                device_id_type=MESH,
            ).start()

    def windows(n, step):
        first, count = STEPS[step]
        arrived(hrecv.at[n, pl.ds(0, 4), :, pl.ds(first, count)], h_r.at[n, step])
        for j, slot in enumerate((0, 1, 4, 2, 3)):
            x = me + j - 2
            inside = jnp.logical_and(x >= 0, x < NS)
            for q in range(2):
                got = hrecv[n, slot, q, first : first + count].astype(F32)
                tmp[j, q, 2 + first : 2 + first + count, :] = jnp.where(inside, got, 0.0)
        for x3 in range(3):
            for blk in range(*BLOCKS[step]):
                lanes = slice((x3 * NB + blk) * 128, (x3 * NB + blk + 1) * 128)
                rows = pl.ds(pl.multiple_of(hy * 16, 16) + blk * BLK, US)
                column = [tmp[x3 + a, q, rows, :] for q in range(2) for a in range(3)]
                vbuf[n, 0 : 6 * US, lanes] = jnp.concatenate(column, axis=0).astype(BF)

    def lanes_of(x3, step):
        lo, hi = BLOCKS[step]
        return slice(x3 * LN + lo * 128, x3 * LN + hi * 128)

    def into_hidden(n, w, step):
        for x3 in range(3):
            lanes = lanes_of(x3, step)
            hid[n, :, lanes] = mm(w[...], vbuf[n, :, lanes])

    x_ok = [jnp.logical_and(me + d >= 0, me + d < NS) for d in (-1, 0, 1)]

    def keep(value, kind, x3, blk):
        if blk == 0:
            value = jnp.where(jnp.logical_and(kind == 1.0, hy == 0), 0.0, value)
        if blk == NB - 1:
            value = jnp.where(jnp.logical_and(kind == 2.0, hy == 1), 0.0, value)
        if x3 != 1:
            value = jnp.where(x_ok[x3], value, 0.0)
        return value

    def out_of_hidden(values, w, step):
        total = mm(w[0], values[:, lanes_of(0, step)])
        total += mm(w[1], values[:, lanes_of(1, step)])
        total += mm(w[2], values[:, lanes_of(2, step)])
        return total

    def gather_send(n, step):
        lo, hi = BLOCKS[step]
        rows = pl.ds(lo * BLK, (hi - lo) * BLK)
        src = agsend.at[n, :, rows]
        dst = agrecv.at[n, co, :, rows]
        pltpu.make_async_copy(src, dst, ag_r.at[n, step]).start()
        for j in range(1, NCOIL):
            to = lax.rem(co + j, NCOIL)
            pltpu.make_async_remote_copy(
                src_ref=src,
                dst_ref=dst,
                send_sem=ag_s.at[n, step],
                recv_sem=ag_r.at[n, step],
                device_id=(me, to),
                device_id_type=MESH,
            ).start()

    def gathered(n):
        for step, (lo, hi) in enumerate(BLOCKS):
            arrived(agrecv.at[n, :, :, pl.ds(lo * BLK, (hi - lo) * BLK)], ag_r.at[n, step])

    def group_sums(rows):
        high = rows.astype(BF)
        rest_of = rows - high.astype(F32)
        middle_part = rest_of.astype(BF)
        low = (rest_of - middle_part.astype(F32)).astype(BF)
        return mm(high, spread[...]) + mm(middle_part, spread[...]) + mm(low, spread[...])

    def second_grad():
        rows_b[...] = jnp.zeros((24, MR), F32)
        own = jnp.concatenate(
            [
                jnp.concatenate(
                    [
                        hrecv[1, 4, q, pl.ds(pl.multiple_of(hy * 16, 16) + blk * BLK, BLK), :]
                        for blk in range(NB)
                    ],
                    axis=1,
                )
                for q in range(2)
            ],
            axis=0,
        )
        for a in range(3):
            cross = mm_nt(own, act[:, a * LN : (a + 1) * LN])
            for q in range(2):
                rows = slice(q * BLK, (q + 1) * BLK)
                for b in range(3):
                    at = a * 6 + b * 2 + q
                    rows_b[at : at + 1, :] = jnp.sum(
                        jnp.where(gap2[rows, :] == float(b), cross[rows, :], 0.0),
                        axis=0,
                        keepdims=True,
                    )
        grads = pltpu.roll(group_sums(rows_b[...]), CH, 1)
        at_row = lax.broadcasted_iota(jnp.int32, (24, 128), 0)
        at_lane = lax.broadcasted_iota(jnp.int32, (24, 128), 1)
        own_f = own.astype(F32)
        for q in range(2):
            spot = jnp.logical_and(at_row == 18, at_lane == CH + q)
            grads += jnp.where(spot, jnp.sum(own_f[q * BLK : (q + 1) * BLK]), 0.0)
        gsec[...] = grads

    arrived(krecv, k_r)
    low_rows = lax.broadcasted_iota(jnp.int32, (8, MR), 0) < 4
    low_lanes = lax.broadcasted_iota(jnp.int32, (8, 128), 1) < 64

    def pick(values, index):
        return jnp.take_along_axis(values, index, axis=1, mode="promise_in_bounds")

    def expand(s, _):
        got = krecv[s].astype(F32)
        halves = []
        for zhi in range(2):
            first = pos[pl.ds(s * 4 + 2 * zhi, 1), :]
            second = pos[pl.ds(s * 4 + 2 * zhi + 1, 1), :]
            index = jnp.where(
                low_rows,
                jnp.broadcast_to(first, (8, MR)),
                jnp.broadcast_to(second, (8, MR)),
            )
            at = [index[:, j * 128 : (j + 1) * 128] for j in range(5)]
            re, im = got[0:8], got[8:16]
            halves.append(
                jnp.concatenate(
                    [
                        pick(re, at[0]),
                        pick(re, at[1]),
                        jnp.where(low_lanes, pick(re, at[2]), pick(im, at[2])),
                        pick(im, at[3]),
                        pick(im, at[4]),
                    ],
                    axis=1,
                )
            )
        ex[pl.ds(pl.multiple_of(s * 16, 16), 16), :] = jnp.concatenate(halves, axis=0).astype(BF)
        return 0

    lax.fori_loop(0, NS, expand, 0, unroll=8)

    def k_y(g, _):
        rows = pl.ds(pl.multiple_of(g * 256, 256), 256)
        half = mm(ex[rows, :], ty[...]).astype(BF).astype(F32)
        for j in range(5):
            hsc[j, rows, :] = half[:, j * 128 : (j + 1) * 128]
        return 0

    lax.fori_loop(0, 4, k_y, 0)
    for j in range(NCH):
        to_image(0, j)
        coil_send(0, j)

    def take_cot(n):
        lo, hi = GROUPS[n]
        arrived(crecv[n], c_r.at[n])
        for j in range(lo, hi):
            lanes = slice((j - lo) * 128, (j - lo + 1) * 128)
            hsc[j] = crecv[n][:, :, lanes].astype(F32).reshape(16 * NS, 128)
            to_image(1, j)
            coil_send(1, j)

    wt[...] = jnp.zeros((2, 128, 128), F32)
    for n, ref in enumerate((first_ref, second_ref)):
        for a in range(3):
            for b in range(3):
                at = (a * 3 + b) * 2
                wt[n, at : at + 2, 0:CH] = ref[a, b].astype(F32)
    w1 = wt[0].astype(BF)
    w2 = wt[1].astype(BF)
    sp = spread[...]
    spt = spread_t[...]
    by_hidden1 = mm_nt(sp, w1).astype(BF)
    by_hidden2 = mm_nt(sp, w2).astype(BF)
    band1 = jnp.zeros((MR, KR), F32)
    band2 = jnp.zeros((MR, KR), F32)
    for b in range(3):
        hit = gap1[...] == float(b)
        band1 += jnp.where(hit, mm(by_hidden1, pick1[b]), 0.0)
        band2 += jnp.where(hit, mm(by_hidden2, pick2[b]), 0.0)
    w1b[...] = band1.astype(BF)
    w2f[...] = band2.astype(BF)
    for a in range(3):
        out2 = jnp.zeros((64, MR), F32)
        out1 = jnp.zeros((64, MR), F32)
        for b in range(3):
            hit = gap2[...] == float(b)
            out2 += jnp.where(hit, mm(mm(rowpick[a * 3 + b], w2).astype(BF), spt), 0.0)
            flipped = rowpick[(2 - a) * 3 + (2 - b)]
            out1 += jnp.where(hit, mm(mm(flipped, w1).astype(BF), spt), 0.0)
        w2b[a] = out2.astype(BF)
        w1f[a] = out1.astype(BF)
    lane = lax.broadcasted_iota(jnp.int32, (1, 128), 1)
    row = jnp.zeros((1, 128), F32)
    for ch in range(CH):
        row = jnp.where(lane == ch, b1_ref[ch], row)
    bias = jnp.sum(sp.astype(F32) * row, axis=1, keepdims=True)
    bcol[...] = jnp.broadcast_to(bias, (MR, 128))
    zero_rows = jnp.zeros((KR - 6 * US, 3 * LN), BF)
    for n in range(2):
        vbuf[n, 6 * US :, :] = zero_rows
    for j in range(5):
        for i in range(2):
            tmp[j, i, 0:8, :] = jnp.zeros((8, 128), F32)
            tmp[j, i, 176:TR, :] = jnp.zeros((TR - 176, 128), F32)

    coil_sum(0, 0)
    coil_sum(0, 1)
    take_cot(0)
    for step in range(2):
        windows(0, step)
        into_hidden(0, w1b, step)
    take_cot(1)
    coil_sum(1, 0)

    def activate(g, _):
        rows = pl.ds(pl.multiple_of(g * 16, 16), 16)
        kind = edge[rows, :]
        add = bcol[rows, :]
        for x3 in range(3):
            for blk in range(NB):
                lanes = slice((x3 * NB + blk) * 128, (x3 * NB + blk + 1) * 128)
                h = hid[0, rows, lanes] + add
                s = 0.5 * jnp.tanh(0.5 * h) + 0.5
                act[rows, lanes] = keep(h * s, kind, x3, blk).astype(BF)
                hid[0, rows, lanes] = s * (1.0 + h * (1.0 - s))
        return 0

    lax.fori_loop(0, MR // 16, activate, 0)
    for step, (lo, hi) in enumerate(BLOCKS):
        regularized = out_of_hidden(act, w2b, step)
        for q in range(2):
            for blk in range(lo, hi):
                lanes = slice((blk - lo) * 128, (blk - lo + 1) * 128)
                block = regularized[q * BLK : (q + 1) * BLK, lanes] + b2_ref[q]
                agsend[0, q, blk * BLK : (blk + 1) * BLK, :] = block.astype(BF)
        gather_send(0, step)

    coil_sum(1, 1)
    second_grad()

    def grad_blocks(step):
        lo, hi = BLOCKS[step]
        windows(1, step)
        into_hidden(1, w2f, step)

        def grad_hidden(g, _):
            rows = pl.ds(pl.multiple_of(g * 16, 16), 16)
            kind = edge[rows, :]
            for x3 in range(3):
                for blk in range(lo, hi):
                    lanes = slice((x3 * NB + blk) * 128, (x3 * NB + blk + 1) * 128)
                    value = hid[1, rows, lanes] * hid[0, rows, lanes]
                    gp[rows, lanes] = keep(value, kind, x3, blk).astype(BF)
            return 0

        lax.fori_loop(0, MR // 16, grad_hidden, 0, unroll=2)
        grad_comb = out_of_hidden(gp, w1f, step)
        for q in range(2):
            for blk in range(lo, hi):
                lanes = slice((blk - lo) * 128, (blk - lo + 1) * 128)
                block = grad_comb[q * BLK : (q + 1) * BLK, lanes]
                agsend[1, q, blk * BLK : (blk + 1) * BLK, :] = block.astype(BF)
        gather_send(1, step)

    grad_blocks(0)
    grad_blocks(1)

    gathered(0)

    def quarters(g):
        for half_y in range(2):
            for half_z in range(2):
                src = pl.ds(pl.multiple_of(g * 16, 16), 16)
                dst = pl.ds(pl.multiple_of(half_y * 160 + g * 16, 16), 16)
                lo = slice(half_z * 128, half_z * 128 + 128)
                hi = slice(NZ + half_z * 128, NZ + half_z * 128 + 128)
                yield half_z * 2 + half_y, src, dst, lo, hi

    def begin(g, _):
        for slot, src, dst, lo, hi in quarters(g):
            r0 = agrecv[0, slot, 0, src, :].astype(F32)
            r1 = agrecv[0, slot, 1, src, :].astype(F32)
            for c in range(CL):
                k0 = img[1, c, dst, lo].astype(F32)
                k1 = img[1, c, dst, hi].astype(F32)
                regpart[0, c, dst, lo] = k0 * r0 + k1 * r1
                regpart[1, c, dst, lo] = k1 * r0 - k0 * r1
        return 0

    rows_a[...] = jnp.zeros((24, MR), F32)
    gp_mid = gp[:, LN : 2 * LN]
    cross = mm_nt(vbuf[0, :, LN : 2 * LN], gp_mid)
    for i in range(2):
        for a in range(3):
            rows = slice((i * 3 + a) * US, (i * 3 + a + 1) * US)
            block = cross[rows, :]
            gap = gap3[rows, :]
            for b in range(3):
                at = (a * 3 + b) * 2 + i
                rows_a[at : at + 1, :] = jnp.sum(
                    jnp.where(gap == float(b), block, 0.0), axis=0, keepdims=True
                )
    sums = mm_nt(jnp.ones((8, LN), BF), gp_mid) * middle[...]
    rows_a[18:19, :] = sums[0:1, :]
    grads = group_sums(rows_a[...])
    grads += gsec[...]
    def share(n, buf, count, mine, device):
        buf[mine] = grads_in[n]
        for j in range(1, count):
            to = lax.rem(mine + j, count)
            pltpu.make_async_remote_copy(
                src_ref=buf.at[mine],
                dst_ref=buf.at[mine],
                send_sem=ar_s.at[n],
                recv_sem=ar_r.at[n],
                device_id=device(to),
                device_id_type=MESH,
            ).start()

    def collect(n, buf, count):
        arrived(buf.at[pl.ds(0, count - 1)], ar_r.at[n])
        total = buf[0]
        for j in range(1, count):
            total += buf[j]
        return total

    grads = grads[0:8] + pltpu.roll(grads[8:16], 36, 1) + pltpu.roll(grads[16:24], 72, 1)
    grads_in = [grads]
    share(0, ar1, 16, row_zc, lambda to: (row_y * 16 + to, co))

    lax.fori_loop(0, 10, begin, 0)
    grads_in.append(collect(0, ar1, 16))
    share(1, ar2, 16, row_y * 4 + co, lambda to: (to // 4 * 16 + row_zc, to % 4))
    gathered(1)

    def result(half):
        def finish(g, _):
            for slot, src, dst, lo, hi in quarters(g):
                g0 = agrecv[1, slot, 0, src, :].astype(F32)
                g1 = agrecv[1, slot, 1, src, :].astype(F32)
                for c in range(half * 2, half * 2 + 2):
                    i0 = img[0, c, dst, lo].astype(F32)
                    i1 = img[0, c, dst, hi].astype(F32)
                    re = i0 * g0 + i1 * g1 - regpart[0, c, dst, lo]
                    im = i1 * g0 - i0 * g1 - regpart[1, c, dst, lo]
                    outv[0, c, dst, lo] = re.astype(BF)
                    outv[1, c, dst, lo] = im.astype(BF)
            return 0

        lax.fori_loop(0, 10, finish, 0)
        for p in range(2):
            store(p, half).start()

    def store(p, half):
        coils = pl.ds(half * 2, 2)
        return pltpu.make_async_copy(
            outv.at[p, coils], pre_hbm.at[p, coils], o_sem.at[p * 2 + half]
        )

    result(0)

    result(1)
    gw_ref[...] = collect(1, ar2, 16) * (1.0 / math.sqrt(NS * NY * NZ))

    arrived(ksend.at[pl.ds(0, NS - 1)], k_s)
    for n in range(len(GROUPS)):
        arrived(csend[n].at[pl.ds(0, NS - 1)], c_s.at[n])
    for n in range(2):
        for step, (first, count) in enumerate(STEPS):
            arrived(rsrecv.at[n, pl.ds(0, 3), :, pl.ds(first, count)], rs_s.at[n, step])
            arrived(hrecv.at[n, pl.ds(0, 4), :, pl.ds(first, count)], h_s.at[n, step])
        for step, (lo, hi) in enumerate(BLOCKS):
            piece = agrecv.at[n, pl.ds(0, NCOIL - 1), :, pl.ds(lo * BLK, (hi - lo) * BLK)]
            arrived(piece, ag_s.at[n, step])
    arrived(ar1.at[pl.ds(0, 15)], ar_s.at[0])
    arrived(ar2.at[pl.ds(0, 15)], ar_s.at[1])
    for p in range(2):
        for half in range(2):
            store(p, half).wait()


def final_kernel(pre_hbm, gw_hbm, out_hbm, g1_hbm, gb1_hbm, g2_hbm, gb2_hbm, *scratch):
    held, folded_ref, g1_ref, gb1_ref, g2_ref, gb2_ref, sem_in, sem_out, sem_small = scratch
    load_g = pltpu.make_async_copy(gw_hbm, folded_ref, sem_small.at[4])
    load_g.start()
    spots = [(p, c) for p in range(2) for c in range(CL)]
    loads = [pltpu.make_async_copy(pre_hbm.at[s], held.at[s], sem_in.at[s]) for s in spots]
    stores = [pltpu.make_async_copy(held.at[s], out_hbm.at[s], sem_out.at[s]) for s in spots]
    for load in loads:
        load.start()
    load_g.wait()
    folded = folded_ref[...]
    first = jnp.concatenate([folded, pltpu.roll(folded, 92, 1), pltpu.roll(folded, 56, 1)], axis=0)
    second = pltpu.roll(first, 128 - CH, 1)
    for a in range(3):
        for b in range(3):
            at = (a * 3 + b) * 2
            g1_ref[a, b] = first[at : at + 2, 0:CH]
            g2_ref[a, b] = second[at : at + 2, 0:CH]
    gb1_ref[...] = first[18:19, 0:CH]
    gb2_ref[...] = second[18:19, 0:2]
    small = [(g1_ref, g1_hbm), (gb1_ref, gb1_hbm), (g2_ref, g2_hbm), (gb2_ref, gb2_hbm)]
    stores += [pltpu.make_async_copy(*pair, sem_small.at[n]) for n, pair in enumerate(small)]
    for store in stores[8:]:
        store.start()
    for load, store in zip(loads, stores):
        load.wait()
        store.start()
    for store in stores:
        store.wait()


def on_device(k_space, cotangent, sens_maps, line_index, w_first, b_first, w_second, b_second):
    constants = make_constants()
    sens = jnp.transpose(sens_maps.reshape(2, CL, NZ, NY), (0, 1, 3, 2))
    index = jnp.transpose(line_index)
    first = jnp.transpose(w_first, (2, 3, 1, 0))
    second = jnp.transpose(w_second, (2, 3, 0, 1))
    vm = pl.BlockSpec(memory_space=pltpu.VMEM)
    anym = pl.BlockSpec(memory_space=pl.ANY)
    dma = pltpu.SemaphoreType.DMA
    scratch = [pltpu.VMEM(c.shape, c.dtype) for c in constants]
    scratch += [
        pltpu.VMEM((2, CL, ZL, NS, NY), BF),
        pltpu.VMEM((2, CL, ZL, NS, NY), BF),
        pltpu.VMEM((2, CL, NY, NZ), BF),
        pltpu.VMEM((16 * NS, 128), F32),
        pltpu.VMEM((NS, 16, 128), BF),
        pltpu.VMEM((NS, 16, 128), BF),
        pltpu.VMEM((5, 16 * NS, 128), F32),
        *[pltpu.VMEM((NS, 16, 128 * (hi - lo)), BF) for lo, hi in GROUPS],
        *[pltpu.VMEM((NS, 16, 128 * (hi - lo)), BF) for lo, hi in GROUPS],
        pltpu.VMEM((NZ, 640), jnp.int32),
        pltpu.VMEM((NZ * CL, 640), BF),
        pltpu.VMEM((5, NZ * CL, 128), F32),
        pltpu.VMEM((2, CL, NY, 2 * NZ), BF),
        pltpu.VMEM((2, 2, NY, NZ), BF),
        pltpu.VMEM((2, NCOIL, 2, PR, 128), BF),
        pltpu.VMEM((2, 5, 2, PR, 128), BF),
        pltpu.VMEM((5, 2, TR, 128), F32),
        pltpu.VMEM((2, KR, 3 * LN), BF),
        pltpu.VMEM((2, MR, 3 * LN), F32),
        pltpu.VMEM((MR, 3 * LN), BF),
        pltpu.VMEM((MR, 3 * LN), BF),
        pltpu.VMEM((MR, 128), F32),
        pltpu.VMEM((MR, KR), BF),
        pltpu.VMEM((MR, KR), BF),
        pltpu.VMEM((3, 64, MR), BF),
        pltpu.VMEM((3, 64, MR), BF),
        pltpu.VMEM((2, 2, NY // 2, 128), BF),
        pltpu.VMEM((2, NCOIL, 2, NY // 2, 128), BF),
        pltpu.VMEM((2, CL, NY, NZ), F32),
        pltpu.VMEM((2, CL, NY, NZ), BF),
        pltpu.VMEM((24, MR), F32),
        pltpu.VMEM((24, MR), F32),
        pltpu.VMEM((24, 128), F32),
        pltpu.VMEM((16, 8, 128), F32),
        pltpu.VMEM((16, 8, 128), F32),
        pltpu.VMEM((LINES, NZ), jnp.int32),
        pltpu.VMEM((3, 3, 2, CH), BF),
        pltpu.VMEM((3, 3, 2, CH), BF),
        pltpu.VMEM((NZ, 128), jnp.int32),
        pltpu.VMEM((NZ, 128), jnp.int32),
        pltpu.VMEM((2, 128, 128), F32),
        dma((6,)),
        dma((len(constants),)),
        dma((4,)),
        dma,
        dma,
        dma((len(GROUPS),)),
        dma((len(GROUPS),)),
        dma((2, 2)),
        dma((2, 2)),
        dma((2, 2)),
        dma((2, 2)),
        dma((2, 2)),
        dma((2, 2)),
        dma((2,)),
        dma((2,)),
    ]
    smem = pl.BlockSpec(memory_space=pltpu.SMEM)
    result, grads = pl.pallas_call(
        cascade_kernel,
        out_shape=(
            jax.ShapeDtypeStruct((2, CL, NY, NZ), BF),
            jax.ShapeDtypeStruct((8, 128), F32),
        ),
        in_specs=[anym] * 6 + [smem] * 2 + [anym] * len(constants),
        out_specs=(anym, vm),
        scratch_shapes=scratch,
        compiler_params=pltpu.CompilerParams(
            collective_id=0, has_side_effects=True, vmem_limit_bytes=60 * 1024 * 1024
        ),
    )(k_space, cotangent, sens, index, first, second, b_first, b_second, *constants)
    grad_sens, grad_w1, grad_b1, grad_w2, grad_b2 = pl.pallas_call(
        final_kernel,
        out_shape=(
            jax.ShapeDtypeStruct((2, CL, NY, NZ), BF),
            jax.ShapeDtypeStruct((3, 3, 2, CH), F32),
            jax.ShapeDtypeStruct((1, CH), F32),
            jax.ShapeDtypeStruct((3, 3, 2, CH), F32),
            jax.ShapeDtypeStruct((1, 2), F32),
        ),
        in_specs=[anym] * 2,
        out_specs=(anym,) * 5,
        scratch_shapes=[
            pltpu.VMEM((2, CL, NY, NZ), BF),
            pltpu.VMEM((8, 128), F32),
            pltpu.VMEM((3, 3, 2, CH), F32),
            pltpu.VMEM((1, CH), F32),
            pltpu.VMEM((3, 3, 2, CH), F32),
            pltpu.VMEM((1, 2), F32),
            dma((2, CL)),
            dma((2, CL)),
            dma((5,)),
        ],
        compiler_params=pltpu.CompilerParams(vmem_limit_bytes=60 * 1024 * 1024),
    )(result, grads)
    grad_sens = jnp.transpose(grad_sens, (0, 1, 3, 2)).reshape(2, CL, NZ, 1, NY)
    grad_w1 = jnp.transpose(grad_w1, (3, 2, 0, 1))
    grad_w2 = jnp.transpose(grad_w2, (2, 3, 0, 1))
    grad_b1 = grad_b1.reshape(CH)
    grad_b2 = grad_b2.reshape(2)
    return (grad_sens, grad_w1, grad_b1, grad_w2, grad_b2)


def solution(mesh):
    placed = (
        P(None, "coil", "space", None, None),
        P(None, "coil", "space", None, None),
        P(None, "coil", None, "space", None),
        P(),
        P(),
        P(),
        P(),
        P(),
    )
    return jax.shard_map(
        on_device,
        mesh=mesh,
        in_specs=placed,
        out_specs=(P(None, "coil", None, "space", None), P(), P(), P(), P()),
        check_vma=False,
    )
```
